256 devices in a mesh: row: 16 (over y, z_hi, core), col: 16 (over x, z_lo).
Axes of the slice: x: 4, y: 4, z: 8 (z_hi: 2, z_lo: 4; z = z_hi * 4 + z_lo), core: 2. Of those that a mesh axis runs over, the one named last changes fastest.
Arguments:
- image: float32 [12288, 1280], P(('row', 'col')), may hold values from -1 to 1
- text: float32 [12288, 1280], P(('col', 'row')), may hold values from -1 to 1
- log_scale: float32 [1], replicated, may hold values from 2 to 3
Outputs:
- loss: float32 [1], replicated
- image_grad: float32 [12288, 1280], P(('row', 'col'))
- text_grad: float32 [12288, 1280], P(('col', 'row'))
- scale_grad: float32 [1], replicated
The draws below stay inside these ranges and needn't reach their ends.
All inputs are finite; a program needn't handle non-finite values.
Results may differ from the reference program's by a relative error of at most 0.0003.
Values sent between devices are 32-bit elements; how exact they have to be, the bound alone decides.
A program may use at most 64 MiB of HBM per device.

```python
import math
import jax
import jax.numpy as jnp
from jax import lax

E = 1280
BATCH = 12288


def draw_common(key):
    return jax.random.normal(jax.random.fold_in(key, 7), (BATCH, E), jnp.float32)


def draw_image(key, part):
    common = draw_common(key)
    key = jax.random.fold_in(key, 1)
    noise_key, gain_key = jax.random.split(key)
    noise = jax.random.normal(noise_key, (BATCH, E), jnp.float32)
    row_gain = jnp.exp(jax.random.uniform(gain_key, (BATCH, 1), jnp.float32, math.log(0.5), math.log(2.0)))
    mixed = (0.55 * common + 0.85 * noise) * row_gain / math.sqrt(E)
    return jnp.clip(mixed, -1.0, 1.0)


def draw_text(key, part):
    common = draw_common(key)
    key = jax.random.fold_in(key, 2)
    noise_key, gain_key = jax.random.split(key)
    noise = jax.random.normal(noise_key, (BATCH, E), jnp.float32)
    row_gain = jnp.exp(jax.random.uniform(gain_key, (BATCH, 1), jnp.float32, math.log(0.5), math.log(2.0)))
    mixed = (0.55 * common + 0.85 * noise) * row_gain / math.sqrt(E)
    return jnp.clip(mixed, -1.0, 1.0)


def setup_inputs(seed: int = 0) -> dict:
    streams_of = jax.random.split(jax.random.key(seed), 4)
    image = draw_image(jax.random.fold_in(streams_of[3], 71), 0)
    text = draw_text(jax.random.fold_in(streams_of[3], 71), 0)
    log_scale = jnp.clip(jax.random.uniform(streams_of[2], (1,), jnp.float32, 2.0, 3.0), 2.0, 3.0)
    return {"image": image, "text": text, "log_scale": log_scale}


def reference(image, text, log_scale):
    logit_scale = jnp.exp(log_scale[0])
    logits = logit_scale * jnp.dot(image, text.T, precision=lax.Precision.HIGHEST, preferred_element_type=jnp.float32)
    row_peak = jnp.max(logits, axis=1)
    row_lse = row_peak + jnp.log(jnp.sum(jnp.exp(logits - row_peak[:, None]), axis=1))
    col_peak = jnp.max(logits, axis=0)
    col_lse = col_peak + jnp.log(jnp.sum(jnp.exp(logits - col_peak[None, :]), axis=0))
    batch_size = image.shape[0]
    identity = jnp.eye(batch_size, dtype=logits.dtype)
    diagonal = jnp.sum(logits * identity)
    loss_value = (jnp.sum(row_lse) + jnp.sum(col_lse) - 2.0 * diagonal) / (2.0 * batch_size)
    weights = 0.5 * (jnp.exp(logits - row_lse[:, None]) + jnp.exp(logits - col_lse[None, :])) - identity
    image_grad = logit_scale * jnp.dot(weights, text, precision=lax.Precision.HIGHEST, preferred_element_type=jnp.float32)
    text_grad = logit_scale * jnp.dot(weights.T, image, precision=lax.Precision.HIGHEST, preferred_element_type=jnp.float32)
    scale_grad = jnp.sum(weights * logits) / batch_size
    return loss_value.reshape(1), image_grad, text_grad, scale_grad.reshape(1)
```

```python
import functools

import jax
import jax.numpy as jnp
from jax import lax
from jax.experimental import pallas as pl
from jax.experimental.pallas import tpu as pltpu
from jax.sharding import PartitionSpec as P

MESH = pl.DeviceIdType.MESH
F32 = jnp.float32
BF16 = jnp.bfloat16

NX, NZ = 4, 8
IMG = [(0, 0), (3, 0), (1, 0), (0, 3), (0, 1),
       (3, 3), (3, 1), (1, 3), (1, 1), (0, 2), (2, 0),
       (3, 2), (2, 3), (1, 2), (2, 1), (2, 2)]
TXT = [(dz, dk) for dz in (0, 7, 1, 6, 2, 5, 3, 4) for dk in (0, 1)]
ISLOT = {p: i for i, p in enumerate(IMG)}
TSLOT = {p: i for i, p in enumerate(TXT)}
PLANE = [(x, y, 0, 0) for x in (2, 3, 1, 0) for y in (2, 3, 1, 0) if (x, y) != (0, 0)]
RING = [(0, 0, z, k) for z in (4, 3, 5, 2, 6, 1, 7, 0) for k in (1, 0) if (z, k) != (0, 0)]
N_COPIES = 192
LN2 = 0.6931471805599453


def position():
    r, c = lax.axis_index("row"), lax.axis_index("col")
    return c // 4, r // 4, ((r // 2) % 2) * 4 + c % 4, r % 2


def shard_of(image, x, y, z, k):
    row, col = (y * 2 + z // 4) * 2 + k, x * 4 + z % 4
    return row * 16 + col if image else col * 16 + row


def split(v):
    hi = v.astype(BF16)
    return hi, (v - hi.astype(F32)).astype(BF16)


def dot3(ah, al, bh, bl, dims):
    d = functools.partial(lax.dot_general, dimension_numbers=(dims, ((), ())), preferred_element_type=F32)
    return d(ah, bh) + (d(al, bh) + d(ah, bl))


def kernel(R, E, batch, im, tx, ls, out_i, out_t, out_loss, out_scale,
           img, txt, ih, il, th, tl, lg, wh, wl, wth, wtl, gi, gt,
           rq, ru, rpq, rpu, rz, rc, cols_a, cols_b, rst, cst, pst, zst, rid, ssem, rsem):
    H = R // 2
    EH = E // 2
    N = 16 * R
    x, y, z, k = position()

    def peer(o):
        px, py, pz, pk = (x + o[0]) % 4, (y + o[1]) % 4, (z + o[2]) % 8, (k + o[3]) % 2
        return ((py * 2 + pz // 4) * 2 + pk, px * 4 + pz % 4)

    copies = []

    def send(src, dst, o):
        i = len(copies)
        c = pltpu.make_async_remote_copy(src_ref=src, dst_ref=dst, send_sem=ssem.at[i], recv_sem=rsem.at[i],
                                         device_id=peer(o), device_id_type=MESH)
        c.start()
        copies.append(c)
        return c

    CORE = (0, 0, 0, 1)

    def zdir(s):
        return (0, 0, s % 8, 0)

    def idir(h, primary, s):
        return (s % 4, 0, 0, 0) if (h == 0) == primary else (0, s % 4, 0, 0)

    def pos(h, p, q):
        p, q = p % 4, q % 4
        return (p, q) if h == 0 else (q, p)

    HALF = {"f": pl.ds(0, E), "A": pl.ds(0, EH), "B": pl.ds(EH, EH)}

    barrier = pltpu.get_barrier_semaphore()
    for o in PLANE + RING:
        pl.semaphore_signal(barrier, inc=1, device_id=peer(o), device_id_type=MESH)
    for s, (dx, dy) in enumerate(IMG):
        rid[s] = shard_of(True, (x + dx) % 4, (y + dy) % 4, z, k) * R
    pl.semaphore_wait(barrier, len(PLANE) + len(RING))

    got = {}

    def isend(h, p, q, primary, s, part="f"):
        o = pos(h, p, q)
        rows = pl.ds(h * H, H)
        src = im.at[rows, HALF[part]] if o == (0, 0) else img.at[ISLOT[o], rows, HALF[part]]
        to = pos(h, p - s, q) if primary else pos(h, p, q - s)
        got[("i", h, to, part)] = send(src, img.at[ISLOT[to], rows, HALF[part]], idir(h, primary, s))

    def iwait(h, p, q):
        o = pos(h, p, q)
        for part in ("f", "A", "B"):
            c = got.pop(("i", h, o, part), None)
            if c is not None:
                c.wait_recv()

    def tsend(dz, s, part):
        rows = pl.ds(0 if part == "a" else H, H)
        src = tx.at[rows, :] if dz == 0 else txt.at[TSLOT[(dz, 0)], rows, :]
        to = (dz - s) % 8
        got[("t", to, part)] = send(src, txt.at[TSLOT[(to, 0)], rows, :], zdir(s))

    def twait(dz, part):
        got.pop(("t", dz, part)).wait_recv()

    def tcore(dz):
        src = tx if dz == 0 else txt.at[TSLOT[(dz, 0)]]
        got[("c", dz)] = send(src, txt.at[TSLOT[(dz, 1)]], CORE)

    def cwait(dz):
        got.pop(("c", dz)).wait_recv()

    def put(hi_ref, lo_ref, s, v):
        rows = pl.ds(s * R if isinstance(s, int) else pl.multiple_of(s * R, R), R)
        hi_ref[rows, :], lo_ref[rows, :] = split(v)

    def conv(ref, hi_ref, lo_ref, a, b):
        def body(s, _):
            put(hi_ref, lo_ref, s, ref[s])
            return 0
        lax.fori_loop(a, b, body, 0)

    scale = jnp.exp(jnp.full((1, 1), ls[0], F32))

    def logits(a, b, t0, t1):
        rows = slice(a * R, b * R)

        def body(t, _):
            cs = pl.ds(pl.multiple_of(t * 256, 256), 256)
            lg[rows, cs] = scale * dot3(ih[rows, :], il[rows, :], th[cs, :], tl[cs, :], ((1,), (1,)))
            return 0
        lax.fori_loop(t0, t1, body, 0)

    for primary in (True, False):
        for h in (0, 1):
            isend(h, 0, 0, primary, 1)
            isend(h, 0, 0, primary, -1)
        if primary:
            for part in ("a", "b"):
                tsend(0, 1, part)
                tsend(0, -1, part)
    tcore(0)
    put(ih, il, 0, im[...])
    put(th, tl, 0, tx[...])

    for h in (0, 1):
        iwait(h, 3, 0)
        iwait(h, 1, 0)
        isend(h, 3, 0, True, 1, "A")
        isend(h, 1, 0, True, -1, "B")
    twait(7, "a")
    twait(1, "a")
    tsend(7, 1, "a")
    tsend(1, -1, "a")
    for h in (0, 1):
        for p in (3, 1):
            isend(h, p, 0, False, 1)
            isend(h, p, 0, False, -1)
    cwait(0)
    for h in (0, 1):
        iwait(h, 0, 3)
        iwait(h, 0, 1)
        isend(h, 0, 3, False, 1, "A")
        isend(h, 0, 1, False, -1, "B")
    twait(7, "b")
    twait(1, "b")
    tsend(7, 1, "b")
    tsend(1, -1, "b")
    tcore(7)
    tcore(1)
    conv(img, ih, il, 1, 5)
    for h in (0, 1):
        iwait(h, 2, 0)
        isend(h, 2, 0, False, 1)
        isend(h, 2, 0, False, -1)
    cwait(7)
    cwait(1)
    conv(txt, th, tl, 1, 6)
    twait(6, "a")
    twait(2, "a")
    tsend(6, 1, "a")
    tsend(2, -1, "a")
    logits(0, 5, 0, 1)
    for h in (0, 1):
        for p in (3,):
            iwait(h, p, 3)
            iwait(h, p, 1)
            isend(h, p, 3, False, 1, "A")
            isend(h, p, 1, False, -1, "B")
    twait(6, "b")
    twait(2, "b")
    tsend(6, 1, "b")
    tsend(2, -1, "b")
    tcore(6)
    tcore(2)
    for h in (0, 1):
        for p in (1,):
            iwait(h, p, 3)
            iwait(h, p, 1)
            isend(h, p, 3, False, 1, "A")
            isend(h, p, 1, False, -1, "B")
    twait(5, "a")
    twait(3, "a")
    tsend(5, 1, "a")
    for h in (0, 1):
        iwait(h, 0, 2)
    conv(img, ih, il, 5, 11)
    logits(5, 11, 0, 1)
    cwait(6)
    cwait(2)
    conv(txt, th, tl, 6, 10)
    for h in (0, 1):
        iwait(h, 2, 3)
        iwait(h, 2, 1)
        isend(h, 2, 3, False, 1, "A")
        isend(h, 2, 1, False, -1, "B")
    twait(5, "b")
    twait(3, "b")
    tsend(3, -1, "b")
    tcore(5)
    tcore(3)
    cwait(5)
    cwait(3)
    conv(txt, th, tl, 10, 14)
    logits(0, 11, 1, 2)
    twait(4, "a")
    twait(4, "b")
    tcore(4)
    for h in (0, 1):
        iwait(h, 3, 2)
        iwait(h, 1, 2)
    conv(img, ih, il, 11, 15)
    cwait(4)
    conv(txt, th, tl, 14, 16)
    logits(0, 11, 2, 3)
    for h in (0, 1):
        iwait(h, 2, 2)
    conv(img, ih, il, 15, 16)
    logits(11, 16, 0, 3)

    RB = 2 * R
    NB = N // RB

    def rows_body(i, cm):
        rows = pl.ds(pl.multiple_of(i * RB, RB), RB)
        v = lg[rows, :]
        rm = jnp.max(v, axis=1, keepdims=True)
        rl = rm + jnp.log(jnp.sum(jnp.exp(v - rm), axis=1, keepdims=True))
        cols_a[rows, :] = jnp.broadcast_to(rl, (RB, 128))
        return jnp.maximum(cm, jnp.max(v.reshape(RB // 8, 8, N), axis=0))

    cm = lax.fori_loop(0, NB, rows_body, jnp.full((8, N), -jnp.inf, F32))
    cm = jnp.max(cm, axis=0, keepdims=True)

    def cols_body(i, cs):
        v = lg[pl.ds(pl.multiple_of(i * RB, RB), RB), :]
        return cs + jnp.sum(jnp.exp(v - cm).reshape(RB // 8, 8, N), axis=0)

    cs = lax.fori_loop(0, NB, cols_body, jnp.zeros((8, N), F32))
    cl = cm + jnp.log(jnp.sum(cs, axis=0, keepdims=True))

    NL = N // 128
    lane = lax.broadcasted_iota(jnp.int32, (128, 128), 1)

    def to_rows(ref):
        m = jnp.zeros((128, 128), F32)
        for b in range(NL):
            m = jnp.where(lane == b, ref[b * 128:(b + 1) * 128, :], m)
        return m.T[:8, :]

    def to_cols(ref, v):
        m = jnp.concatenate([v, jnp.zeros((120, 128), F32)], axis=0).T
        for b in range(NL):
            ref[b * 128:(b + 1) * 128, :] = jnp.broadcast_to(m[:, b:b + 1], (128, 128))

    def iabs(s):
        return ((x + IMG[s][0]) % 4) * 4 + (y + IMG[s][1]) % 4

    def tabs(s):
        return ((z + TXT[s][0]) % 8) * 2 + (k + TXT[s][1]) % 2

    def to_abs(where):
        for s in range(16):
            cols_b[pl.ds(pl.multiple_of(where(s) * R, R), R), :] = cols_a[s * R:(s + 1) * R, :]

    def to_rel(where):
        for s in range(16):
            cols_a[s * R:(s + 1) * R, :] = cols_b[pl.ds(pl.multiple_of(where(s) * R, R), R), :]

    me_p, me_r = x * 4 + y, z * 2 + k
    to_abs(iabs)
    rst[me_p] = to_rows(cols_b)
    plane = [send(rst.at[me_p], rst.at[me_p], o) for o in PLANE]
    c8 = jnp.concatenate([cl[:, b * 128:(b + 1) * 128] for b in range(NL)] + [jnp.zeros((8 - NL, 128), F32)], axis=0)
    to_cols(cols_a, c8)
    to_abs(tabs)
    cst[me_r] = to_rows(cols_b)
    ring = [send(cst.at[me_r], cst.at[me_r], o) for o in RING]

    def merge(ref):
        v = ref[...]
        m = jnp.max(v, axis=0)
        return m + jnp.log(jnp.sum(jnp.exp(v - m[None]), axis=0))

    lane_n = lax.broadcasted_iota(jnp.int32, (1, N), 1)
    cid = lane_n
    for s, (dz, dk) in enumerate(TXT):
        base = shard_of(False, x, y, (z + dz) % 8, (k + dk) % 2) * R - s * R
        cid = jnp.where((lane_n >= s * R) & (lane_n < (s + 1) * R), lane_n + base, cid)

    for c in ring:
        c.wait_recv()
    to_cols(cols_b, merge(cst))
    to_rel(tabs)
    c8 = to_rows(cols_a)
    cl = jnp.concatenate([c8[b:b + 1, :] for b in range(NL)], axis=1)
    for c in plane:
        c.wait_recv()
    to_cols(cols_b, merge(rst))
    to_rel(iabs)
    col_sum = jnp.sum(jnp.where(lane_n < R, cl, 0.0))
    row_sum = jnp.sum(cols_a[0:R, 0:1])
    cl2 = cl + LN2

    sub = lax.broadcasted_iota(jnp.int32, (R, N), 0)

    def weights(s):
        rows = pl.ds(pl.multiple_of(s * R, R), R)
        v = lg[rows, :]
        w = jnp.exp(v - (cols_a[rows, 0:1] + LN2)) + jnp.exp(v - cl2)
        hit = (cid - rid[s]) == sub
        return rows, v, hit, jnp.where(hit, w - 1.0, w)

    def weights_body(s, _):
        rows, v, hit, w = weights(s)
        wh[rows, :], wl[rows, :] = split(w)
        return 0

    lax.fori_loop(0, 16, weights_body, 0)

    def transpose(b0, b1):
        def body(b, _):
            cs = pl.ds(pl.multiple_of(b * 128, 128), 128)
            wth[cs, :] = wh[:, cs].T
            wtl[cs, :] = wl[:, cs].T
            return 0
        lax.fori_loop(b0, b1, body, 0)

    def product(dst, ah, al, bh, bl, a, b):
        rows = slice(a * R, b * R)

        def body(n, _):
            cs = pl.ds(pl.multiple_of(n * 256, 256), 256)
            dst[rows, cs] = dot3(ah[rows, :], al[rows, :], bh[:, cs], bl[:, cs], ((1,), (0,)))
            return 0
        lax.fori_loop(0, E // 256, body, 0)

    def image_product(a, b):
        product(gi, wh, wl, th, tl, a, b)

    def text_product(a, b):
        product(gt, wth, wtl, ih, il, a, b)

    COL = {"f": slice(0, E), "A": slice(0, EH), "B": slice(EH, E)}
    red = {}

    def grows(h, o):
        return ISLOT[o] * R + h * H

    def quarter(h, p):
        o = pos(h, p, 2)
        r = pl.ds(grows(h, o), H)
        red[("q", h, p, 1)] = send(gi.at[r, HALF["A"]], rq.at[h, p, 0], idir(h, False, 1))
        red[("q", h, p, 3)] = send(gi.at[r, HALF["B"]], rq.at[h, p, 1], idir(h, False, -1))

    def unit(h, p):
        for q, part, j, s in ((1, "A", 0, 1), (3, "B", 1, -1)):
            red.pop(("q", h, p, q)).wait_recv()
            a = grows(h, pos(h, p, q))
            gi[a:a + H, COL[part]] += rq[h, p, j]
            red[("u", h, p, q)] = send(gi.at[pl.ds(a, H), :], ru.at[h, p, j], idir(h, False, s))

    def gathered(h, p):
        a = grows(h, pos(h, p, 0))
        for q in (1, 3):
            red.pop(("u", h, p, q)).wait_recv()
        gi[a:a + H, :] += ru[h, p, 0] + ru[h, p, 1]

    def pquarter(h):
        r = pl.ds(grows(h, pos(h, 2, 0)), H)
        red[("pq", h, 1)] = send(gi.at[r, HALF["A"]], rpq.at[h, 0], idir(h, True, 1))
        red[("pq", h, 3)] = send(gi.at[r, HALF["B"]], rpq.at[h, 1], idir(h, True, -1))

    def punit(h):
        for p, part, j, s in ((1, "A", 0, 1), (3, "B", 1, -1)):
            red.pop(("pq", h, p)).wait_recv()
            a = grows(h, pos(h, p, 0))
            gi[a:a + H, COL[part]] += rpq[h, j]
            red[("pu", h, p)] = send(gi.at[pl.ds(a, H), :], rpu.at[h, j], idir(h, True, s))

    def image_out(h):
        for p in (1, 3):
            red.pop(("pu", h, p)).wait_recv()
        a = grows(h, (0, 0))
        out_i[h * H:(h + 1) * H, :] = scale * (gi[a:a + H, :] + (rpu[h, 0] + rpu[h, 1]))

    ZR = {"a": 0, "b": H}

    def core_send(dz):
        red[("c", dz)] = send(gt.at[pl.ds(TSLOT[(dz, 1)] * R, R), :], rc.at[dz], CORE)

    def core_add(dz):
        red.pop(("c", dz)).wait_recv()
        a = TSLOT[(dz, 0)] * R
        gt[a:a + R, :] += rc[dz]

    def zsend(dz, s, part):
        a = TSLOT[(dz, 0)] * R + ZR[part]
        to = (dz - s) % 8
        j = 0 if part == "a" else 1
        red[("z", to, s, part)] = send(gt.at[pl.ds(a, H), :], rz.at[dz, j], zdir(s))

    def zadd(dz, s, part):
        red.pop(("z", dz, s, part)).wait_recv()
        a = TSLOT[(dz, 0)] * R + ZR[part]
        j = 0 if part == "a" else 1
        gt[a:a + H, :] += rz[(dz + s) % 8, j]

    transpose(NL // 2, NL)
    text_product(10, 16)
    for dz in (4, 3, 5):
        core_send(dz)
    image_product(11, 16)
    for h in (0, 1):
        quarter(h, 2)
    core_add(4)
    zsend(4, 1, "a")
    zsend(4, -1, "b")
    for p in (3, 1):
        for h in (0, 1):
            quarter(h, p)
    core_add(3)
    core_add(5)
    zsend(3, 1, "b")
    zsend(5, -1, "a")
    image_product(5, 11)
    for h in (0, 1):
        unit(h, 2)
    for h in (0, 1):
        quarter(h, 0)
    transpose(0, NL // 2)
    text_product(6, 10)
    for dz in (2, 6):
        core_send(dz)
    zadd(3, 1, "a")
    zsend(3, 1, "a")
    zadd(5, -1, "b")
    zsend(5, -1, "b")
    for p in (3, 1):
        for h in (0, 1):
            unit(h, p)
    core_add(2)
    core_add(6)
    text_product(0, 6)
    for dz in (1, 7, 0):
        core_send(dz)
    zadd(2, 1, "b")
    zsend(2, 1, "b")
    zadd(6, -1, "a")
    zsend(6, -1, "a")
    image_product(0, 5)
    for h in (0, 1):
        gathered(h, 2)
        pquarter(h)
    zadd(2, 1, "a")
    zsend(2, 1, "a")
    zadd(6, -1, "b")
    zsend(6, -1, "b")
    for dz in (1, 7, 0):
        core_add(dz)
    for h in (0, 1):
        unit(h, 0)

    def sums_body(s, c):
        rows, v, hit, w = weights(s)
        a, d = c
        a = a + jnp.sum((w * v).reshape(R // 8, 8, N), axis=0)
        d = d + jnp.sum(jnp.where(hit, v, 0.0).reshape(R // 8, 8, N), axis=0)
        return a, d

    zero = jnp.zeros((8, N), F32)
    sw, sd = lax.fori_loop(0, 16, sums_body, (zero, zero))
    scale_part = jnp.sum(sw) / batch
    loss_part = (row_sum + col_sum - 2.0 * jnp.sum(sd)) / (2.0 * batch)
    sub8 = lax.broadcasted_iota(jnp.int32, (8, 128), 0)
    pst[me_p] = jnp.where(sub8 == 0, loss_part, jnp.where(sub8 == 1, scale_part, 0.0))
    plane = [send(pst.at[me_p], pst.at[me_p], o) for o in PLANE]

    zadd(1, 1, "b")
    zsend(1, 1, "b")
    zadd(7, -1, "a")
    zsend(7, -1, "a")
    for h in (0, 1):
        gathered(h, 3)
        gathered(h, 1)
        punit(h)
    zadd(1, 1, "a")
    zsend(1, 1, "a")
    zadd(7, -1, "b")
    zsend(7, -1, "b")
    for c in plane:
        c.wait_recv()
    zst[me_r] = jnp.sum(pst[...], axis=0)
    ring = [send(zst.at[me_r], zst.at[me_r], o) for o in RING]
    for h in (0, 1):
        gathered(h, 0)
    zadd(0, 1, "b")
    zadd(0, -1, "a")
    for c in ring:
        c.wait_recv()
    total = jnp.sum(zst[...], axis=0)
    out_loss[0] = jnp.max(total[0:1, 0:1])
    out_scale[0] = jnp.max(total[1:2, 0:1])
    zadd(0, 1, "a")
    zadd(0, -1, "b")
    out_t[...] = scale * gt[0:R, :]
    for h in (0, 1):
        image_out(h)
    for c in copies:
        c.wait_send()


def per_device(image, text, log_scale):
    R, E = image.shape
    N = 16 * R
    batch = 256 * R
    H, EH = R // 2, E // 2
    vm = pltpu.VMEM
    vspec = pl.BlockSpec(memory_space=pltpu.VMEM)
    sspec = pl.BlockSpec(memory_space=pltpu.SMEM)
    one = jax.ShapeDtypeStruct((1,), F32)
    gi, gt, loss, sg = pl.pallas_call(
        functools.partial(kernel, R, E, float(batch)),
        out_shape=(jax.ShapeDtypeStruct((R, E), F32), jax.ShapeDtypeStruct((R, E), F32), one, one),
        in_specs=[vspec, vspec, sspec],
        out_specs=(vspec, vspec, sspec, sspec),
        scratch_shapes=[
            vm((16, R, E), F32), vm((16, R, E), F32),
            vm((N, E), BF16), vm((N, E), BF16), vm((N, E), BF16), vm((N, E), BF16),
            vm((N, N), F32), vm((N, N), BF16), vm((N, N), BF16), vm((N, N), BF16), vm((N, N), BF16),
            vm((N, E), F32), vm((N, E), F32),
            vm((2, 4, 2, H, EH), F32), vm((2, 4, 2, H, E), F32),
            vm((2, 2, H, EH), F32), vm((2, 2, H, E), F32),
            vm((8, 2, H, E), F32), vm((8, R, E), F32),
            vm((N, 128), F32), vm((N, 128), F32),
            vm((16, 8, 128), F32), vm((16, 8, 128), F32), vm((16, 8, 128), F32), vm((16, 8, 128), F32),
            pltpu.SMEM((16,), jnp.int32),
            pltpu.SemaphoreType.DMA((N_COPIES,)), pltpu.SemaphoreType.DMA((N_COPIES,)),
        ],
        compiler_params=pltpu.CompilerParams(collective_id=0, has_side_effects=True, vmem_limit_bytes=60 * 2**20),
        cost_estimate=pl.CostEstimate(flops=18 * N * N * E, bytes_accessed=16 * R * E, transcendentals=6 * N * N),
    )(image, text, log_scale)
    return loss, gi, gt, sg


def solution(mesh):
    return jax.shard_map(
        per_device,
        mesh=mesh,
        in_specs=(P(("row", "col"), None), P(("col", "row"), None), P()),
        out_specs=(P(), P(("row", "col"), None), P(("col", "row"), None), P()),
        check_vma=False,
    )
```

```python
import functools

import jax
import jax.numpy as jnp
from jax import lax
from jax.experimental import pallas as pl
from jax.experimental.pallas import tpu as pltpu
from jax.sharding import PartitionSpec as P

MESH = pl.DeviceIdType.MESH
F32 = jnp.float32
BF16 = jnp.bfloat16

NX, NZ = 4, 8
IMG = [(0, 0), (3, 0), (1, 0), (0, 3), (0, 1),
       (3, 3), (3, 1), (1, 3), (1, 1), (0, 2), (2, 0),
       (3, 2), (2, 3), (1, 2), (2, 1), (2, 2)]
TXT = [(dz, dk) for dz in (0, 7, 1, 6, 2, 5, 3, 4) for dk in (0, 1)]
ISLOT = {p: i for i, p in enumerate(IMG)}
TSLOT = {p: i for i, p in enumerate(TXT)}
PLANE = [(x, y, 0, 0) for x in (2, 3, 1, 0) for y in (2, 3, 1, 0) if (x, y) != (0, 0)]
RING = [(0, 0, z, k) for z in (4, 3, 5, 2, 6, 1, 7, 0) for k in (1, 0) if (z, k) != (0, 0)]
N_COPIES = 208
CHUNK = {0: (0, 16), 1: (16, 16), 2: (32, 16), "p": (16, 8), "m": (24, 8)}


def position():
    r, c = lax.axis_index("row"), lax.axis_index("col")
    return c // 4, r // 4, ((r // 2) % 2) * 4 + c % 4, r % 2


def shard_of(image, x, y, z, k):
    row, col = (y * 2 + z // 4) * 2 + k, x * 4 + z % 4
    return row * 16 + col if image else col * 16 + row


def split(v):
    hi = v.astype(BF16)
    return hi, (v - hi.astype(F32)).astype(BF16)


def dot3(ah, al, bh, bl, dims):
    d = functools.partial(lax.dot_general, dimension_numbers=(dims, ((), ())), preferred_element_type=F32)
    return d(ah, bh) + (d(al, bh) + d(ah, bl))


def kernel(R, E, batch, im, tx, ls_hbm, out_i, out_t, out_s,
           img, txt, ih, il, th, tl, lg, er, ec, wh, wl, wth, wtl, gi, gt,
           rq, ru, rpq, rpu, rz, rc, cols_a, cols_b, row_max, row_dot, rst, cst, pst, zst, ls, rid, lsem, ssem, rsem):
    H = R // 2
    EH = E // 2
    N = 16 * R
    x, y, z, k = position()

    def peer(o):
        px, py, pz, pk = (x + o[0]) % 4, (y + o[1]) % 4, (z + o[2]) % 8, (k + o[3]) % 2
        return ((py * 2 + pz // 4) * 2 + pk, px * 4 + pz % 4)

    copies = []

    def send(src, dst, o):
        i = len(copies)
        c = pltpu.make_async_remote_copy(src_ref=src, dst_ref=dst, send_sem=ssem.at[i], recv_sem=rsem.at[i],
                                         device_id=peer(o), device_id_type=MESH)
        c.start()
        copies.append(c)
        return c

    CORE = (0, 0, 0, 1)

    def zdir(s):
        return (0, 0, s % 8, 0)

    def idir(h, primary, s):
        return (s % 4, 0, 0, 0) if (h == 0) == primary else (0, s % 4, 0, 0)

    def pos(h, p, q):
        p, q = p % 4, q % 4
        return (p, q) if h == 0 else (q, p)

    HALF = {"f": pl.ds(0, E), "A": pl.ds(0, EH), "B": pl.ds(EH, EH)}

    barrier = pltpu.get_barrier_semaphore()
    for o in PLANE + RING:
        pl.semaphore_signal(barrier, inc=1, device_id=peer(o), device_id_type=MESH)
    local = [pltpu.make_async_copy(im, img.at[0], lsem.at[0]), pltpu.make_async_copy(tx, txt.at[0], lsem.at[1]),
             pltpu.make_async_copy(ls_hbm, ls, lsem.at[2])]
    for c in local:
        c.start()
    for s, (dx, dy) in enumerate(IMG):
        rid[s] = shard_of(True, (x + dx) % 4, (y + dy) % 4, z, k) * R
    for c in local:
        c.wait()
    pl.semaphore_wait(barrier, len(PLANE) + len(RING))

    got = {}

    def isend(h, p, q, primary, s, part="f"):
        o = pos(h, p, q)
        rows = pl.ds(h * H, H)
        src = img.at[ISLOT[o], rows, HALF[part]]
        to = pos(h, p - s, q) if primary else pos(h, p, q - s)
        got[("i", h, to, part)] = send(src, img.at[ISLOT[to], rows, HALF[part]], idir(h, primary, s))

    def iwait(h, p, q):
        o = pos(h, p, q)
        for part in ("f", "A", "B"):
            c = got.pop(("i", h, o, part), None)
            if c is not None:
                c.wait_recv()

    def tsend(dz, s, ch):
        rows = pl.ds(*CHUNK[ch])
        to = (dz - s) % 8
        got[("t", to, ch)] = send(txt.at[TSLOT[(dz, 0)], rows, :], txt.at[TSLOT[(to, 0)], rows, :], zdir(s))

    def tpass(d, ch):
        for dz, s in ((8 - d, 1), (d, -1)):
            got.pop(("t", dz, ch)).wait_recv()
            nxt = ch if d < 3 else {(1, 0): 0, (1, 1): "p", (-1, 1): "m", (-1, 2): 2}.get((s, ch))
            if nxt is not None:
                tsend(dz, s, nxt)

    def tlast():
        for ch in (0, "p", "m", 2):
            got.pop(("t", 4, ch)).wait_recv()

    def tcore(dz):
        got[("c", dz)] = send(txt.at[TSLOT[(dz, 0)]], txt.at[TSLOT[(dz, 1)]], CORE)

    def cwait(dz):
        got.pop(("c", dz)).wait_recv()

    def put(hi_ref, lo_ref, s, v):
        rows = pl.ds(s * R if isinstance(s, int) else pl.multiple_of(s * R, R), R)
        hi_ref[rows, :], lo_ref[rows, :] = split(v)

    def conv(ref, hi_ref, lo_ref, a, b):
        def body(s, _):
            put(hi_ref, lo_ref, s, ref[s])
            return 0
        lax.fori_loop(a, b, body, 0)

    scale = jnp.exp(jnp.full((1, 1), ls[0], F32))

    def logits(a, b, t0, t1):
        rows = slice(a * R, b * R)

        def body(t, _):
            cs = pl.ds(pl.multiple_of(t * 256, 256), 256)
            lg[rows, cs] = scale * dot3(ih[rows, :], il[rows, :], th[cs, :], tl[cs, :], ((1,), (1,)))
            return 0
        lax.fori_loop(t0, t1, body, 0)

    def ipass(h, p, q, primary, s):
        isend(h, p, q, primary, s, "A" if s == 1 else "B")

    def second(p):
        for h in (0, 1):
            iwait(h, p, 3)
            ipass(h, p, 3, False, 1)
            iwait(h, p, 1)
            ipass(h, p, 1, False, -1)

    def third(p):
        for h in (0, 1):
            iwait(h, p, 2)

    for h in (0, 1):
        isend(h, 0, 0, True, 1)
        isend(h, 0, 0, True, -1)
    for ch in (0, 1, 2):
        tsend(0, 1, ch)
        tsend(0, -1, ch)
    for h in (0, 1):
        isend(h, 0, 0, False, 1)
        isend(h, 0, 0, False, -1)
    tcore(0)
    put(ih, il, 0, img[0])
    put(th, tl, 0, txt[0])

    tpass(1, 0)
    for h in (0, 1):
        iwait(h, 3, 0)
        ipass(h, 3, 0, True, 1)
        iwait(h, 1, 0)
        ipass(h, 1, 0, True, -1)
    for p in (3, 1):
        for h in (0, 1):
            isend(h, p, 0, False, 1)
            isend(h, p, 0, False, -1)
    tpass(1, 1)
    second(0)
    tpass(1, 2)
    tcore(7)
    tcore(1)
    for h in (0, 1):
        iwait(h, 2, 0)
        isend(h, 2, 0, False, 1)
        isend(h, 2, 0, False, -1)
    conv(img, ih, il, 1, 5)
    tpass(2, 0)
    for dz in (0, 7, 1):
        cwait(dz)
    conv(txt, th, tl, 1, 6)
    tpass(2, 1)
    logits(0, 5, 0, 1)
    second(3)
    tpass(2, 2)
    tcore(6)
    tcore(2)
    second(1)
    tpass(3, 0)
    cwait(6)
    cwait(2)
    conv(img, ih, il, 5, 9)
    third(0)
    tpass(3, 1)
    conv(txt, th, tl, 6, 10)
    second(2)
    tpass(3, 2)
    tcore(5)
    tcore(3)
    conv(img, ih, il, 9, 11)
    logits(5, 11, 0, 1)
    third(3)
    cwait(5)
    cwait(3)
    conv(txt, th, tl, 10, 14)
    logits(0, 11, 1, 2)
    tlast()
    tcore(4)
    third(1)
    conv(img, ih, il, 11, 15)
    logits(11, 15, 0, 2)
    cwait(4)
    conv(txt, th, tl, 14, 16)
    logits(0, 15, 2, 3)
    third(2)
    conv(img, ih, il, 15, 16)
    logits(15, 16, 0, 3)

    RB = 2 * R
    NB = N // RB

    def rows_body(i, cm):
        rows = pl.ds(pl.multiple_of(i * RB, RB), RB)
        v = lg[rows, :]
        rm = jnp.max(v, axis=1, keepdims=True)
        e = jnp.exp(v - rm)
        er[rows, :] = e
        row_max[rows, :] = jnp.broadcast_to(rm, (RB, 128))
        rl = rm + jnp.log(jnp.sum(e, axis=1, keepdims=True))
        cols_a[rows, :] = jnp.broadcast_to(rl, (RB, 128))
        return jnp.maximum(cm, jnp.max(v.reshape(RB // 8, 8, N), axis=0))

    cm = lax.fori_loop(0, NB, rows_body, jnp.full((8, N), -jnp.inf, F32))
    cm = jnp.max(cm, axis=0, keepdims=True)

    def cols_body(i, cs):
        rows = pl.ds(pl.multiple_of(i * RB, RB), RB)
        e = jnp.exp(lg[rows, :] - cm)
        ec[rows, :] = e
        return cs + jnp.sum(e.reshape(RB // 8, 8, N), axis=0)

    NL = N // 128
    lane = lax.broadcasted_iota(jnp.int32, (128, 128), 1)

    def to_rows(ref):
        m = jnp.zeros((128, 128), F32)
        for b in range(NL):
            m = jnp.where(lane == b, ref[b * 128:(b + 1) * 128, :], m)
        return m.T[:8, :]

    def to_cols(ref, v):
        m = jnp.concatenate([v, jnp.zeros((120, 128), F32)], axis=0).T
        for b in range(NL):
            ref[b * 128:(b + 1) * 128, :] = jnp.broadcast_to(m[:, b:b + 1], (128, 128))

    def iabs(s):
        return ((x + IMG[s][0]) % 4) * 4 + (y + IMG[s][1]) % 4

    def tabs(s):
        return ((z + TXT[s][0]) % 8) * 2 + (k + TXT[s][1]) % 2

    def to_abs(where):
        for s in range(16):
            cols_b[pl.ds(pl.multiple_of(where(s) * R, R), R), :] = cols_a[s * R:(s + 1) * R, :]

    def to_rel(where):
        for s in range(16):
            cols_a[s * R:(s + 1) * R, :] = cols_b[pl.ds(pl.multiple_of(where(s) * R, R), R), :]

    me_p, me_r = x * 4 + y, z * 2 + k
    to_abs(iabs)
    rst[me_p] = to_rows(cols_b)
    plane = [send(rst.at[me_p], rst.at[me_p], o) for o in PLANE]
    cs = lax.fori_loop(0, NB, cols_body, jnp.zeros((8, N), F32))
    cl = cm + jnp.log(jnp.sum(cs, axis=0, keepdims=True))
    c8 = jnp.concatenate([cl[:, b * 128:(b + 1) * 128] for b in range(NL)] + [jnp.zeros((8 - NL, 128), F32)], axis=0)
    to_cols(cols_a, c8)
    to_abs(tabs)
    cst[me_r] = to_rows(cols_b)
    ring = [send(cst.at[me_r], cst.at[me_r], o) for o in RING]

    def merge(ref):
        v = ref[...]
        m = jnp.max(v, axis=0)
        return m + jnp.log(jnp.sum(jnp.exp(v - m[None]), axis=0))

    lane_n = lax.broadcasted_iota(jnp.int32, (1, N), 1)
    cid = lane_n
    for s, (dz, dk) in enumerate(TXT):
        base = shard_of(False, x, y, (z + dz) % 8, (k + dk) % 2) * R - s * R
        cid = jnp.where((lane_n >= s * R) & (lane_n < (s + 1) * R), lane_n + base, cid)

    sub = lax.broadcasted_iota(jnp.int32, (R, N), 0)

    def tile_rows(s):
        rows = pl.ds(pl.multiple_of(s * R, R), R)
        return rows, (cid - rid[s]) == sub

    def dots_body(s, c):
        rows, hit = tile_rows(s)
        v = lg[rows, :]
        a, d = c
        row_dot[rows, :] = jnp.broadcast_to(jnp.sum(er[rows, :] * v, axis=1, keepdims=True), (R, 128))
        a = a + jnp.sum((ec[rows, :] * v).reshape(R // 8, 8, N), axis=0)
        d = d + jnp.sum(jnp.where(hit, v, 0.0).reshape(R // 8, 8, N), axis=0)
        return a, d

    zero = jnp.zeros((8, N), F32)
    col_dot, diag = lax.fori_loop(0, 16, dots_body, (zero, zero))
    col_dot = jnp.sum(col_dot, axis=0, keepdims=True)
    diag = jnp.sum(diag)

    for c in plane:
        c.wait_recv()
    to_cols(cols_b, merge(rst))
    to_rel(iabs)
    row_sum = jnp.sum(cols_a[0:R, 0:1])
    row_max[...] = 0.5 * jnp.exp(row_max[...] - cols_a[...])
    for c in ring:
        c.wait_recv()
    to_cols(cols_b, merge(cst))
    to_rel(tabs)
    c8 = to_rows(cols_a)
    cl = jnp.concatenate([c8[b:b + 1, :] for b in range(NL)], axis=1)
    fc = 0.5 * jnp.exp(cm - cl)

    def weights_body(s, _):
        rows, hit = tile_rows(s)
        w = er[rows, :] * row_max[rows, 0:1] + ec[rows, :] * fc
        wh[rows, :], wl[rows, :] = split(jnp.where(hit, w - 1.0, w))
        return 0

    lax.fori_loop(0, 16, weights_body, 0)

    def transpose(b0, b1):
        def body(b, _):
            cs = pl.ds(pl.multiple_of(b * 128, 128), 128)
            wth[cs, :] = wh[:, cs].T
            wtl[cs, :] = wl[:, cs].T
            return 0
        lax.fori_loop(b0, b1, body, 0)

    def product(dst, ah, al, bh, bl, a, b):
        rows = slice(a * R, b * R)

        def body(n, _):
            cs = pl.ds(pl.multiple_of(n * (E // 2), 128), E // 2)
            dst[rows, cs] = dot3(ah[rows, :], al[rows, :], bh[:, cs], bl[:, cs], ((1,), (0,)))
            return 0
        lax.fori_loop(0, 2, body, 0)

    def image_product(a, b):
        product(gi, wh, wl, th, tl, a, b)

    def text_product(a, b):
        product(gt, wth, wtl, ih, il, a, b)

    COL = {"f": slice(0, E), "A": slice(0, EH), "B": slice(EH, E)}
    red = {}

    def grows(h, o):
        return ISLOT[o] * R + h * H

    def quarter(h, p):
        o = pos(h, p, 2)
        r = pl.ds(grows(h, o), H)
        red[("q", h, p, 1)] = send(gi.at[r, HALF["A"]], rq.at[h, p, 0], idir(h, False, 1))
        red[("q", h, p, 3)] = send(gi.at[r, HALF["B"]], rq.at[h, p, 1], idir(h, False, -1))

    def unit(h, p):
        for q, part, j, s in ((1, "A", 0, 1), (3, "B", 1, -1)):
            red.pop(("q", h, p, q)).wait_recv()
            a = grows(h, pos(h, p, q))
            gi[a:a + H, COL[part]] += rq[h, p, j]
            red[("u", h, p, q)] = send(gi.at[pl.ds(a, H), :], ru.at[h, p, j], idir(h, False, s))

    def gathered(h, p):
        a = grows(h, pos(h, p, 0))
        for q in (1, 3):
            red.pop(("u", h, p, q)).wait_recv()
        gi[a:a + H, :] += ru[h, p, 0] + ru[h, p, 1]

    def pquarter(h):
        r = pl.ds(grows(h, pos(h, 2, 0)), H)
        red[("pq", h, 1)] = send(gi.at[r, HALF["A"]], rpq.at[h, 0], idir(h, True, 1))
        red[("pq", h, 3)] = send(gi.at[r, HALF["B"]], rpq.at[h, 1], idir(h, True, -1))

    def punit(h):
        for p, part, j, s in ((1, "A", 0, 1), (3, "B", 1, -1)):
            red.pop(("pq", h, p)).wait_recv()
            a = grows(h, pos(h, p, 0))
            gi[a:a + H, COL[part]] += rpq[h, j]
            red[("pu", h, p)] = send(gi.at[pl.ds(a, H), :], rpu.at[h, j], idir(h, True, s))

    def image_out(h):
        for p in (1, 3):
            red.pop(("pu", h, p)).wait_recv()
        a = grows(h, (0, 0))
        out_i[h * H:(h + 1) * H, :] = scale * (gi[a:a + H, :] + (rpu[h, 0] + rpu[h, 1]))

    def core_send(dz):
        red[("c", dz)] = send(gt.at[pl.ds(TSLOT[(dz, 1)] * R, R), :], rc.at[dz], CORE)

    def core_add(dz):
        red.pop(("c", dz)).wait_recv()
        a = TSLOT[(dz, 0)] * R
        gt[a:a + R, :] += rc[dz]

    def zsend(dz, s, ch):
        a, n = CHUNK[ch]
        src = gt.at[pl.ds(TSLOT[(dz, 0)] * R + a, n), :]
        red[("z", (dz - s) % 8, s, ch)] = send(src, rz.at[dz, pl.ds(a, n), :], zdir(s))

    def zadd(dz, s, ch):
        red.pop(("z", dz, s, ch)).wait_recv()
        a, n = CHUNK[ch]
        g = TSLOT[(dz, 0)] * R + a
        gt[g:g + n, :] += rz[(dz + s) % 8, a:a + n, :]

    def zstep(d, j):
        for dz, s, ch in ((d, 1, (2, 0, 1)[j]), (8 - d, -1, (0, 2, 1)[j])):
            if d == 3:
                came = None if j == 0 else ch if j == 1 else ("p" if s == 1 else "m")
            else:
                came = ch
            if came is not None:
                zadd(dz % 8, s, came)
            if d > 0:
                zsend(dz, s, ch)

    transpose(NL - 1, NL)
    text_product(14, 16)
    core_send(4)
    image_product(11, 16)
    for p in (2, 3, 1):
        for h in (0, 1):
            quarter(h, p)
    core_add(4)
    for s, ch in ((1, 0), (-1, 2), (1, "p"), (-1, "m")):
        zsend(4, s, ch)
    transpose(NL // 2, NL - 1)
    text_product(10, 14)
    for dz in (3, 5):
        core_send(dz)
    for h in (0, 1):
        unit(h, 2)
    for dz in (3, 5):
        core_add(dz)
    zstep(3, 0)
    image_product(5, 11)
    for h in (0, 1):
        quarter(h, 0)
    zstep(3, 1)
    for p in (3, 1):
        for h in (0, 1):
            unit(h, p)
    zstep(3, 2)

    scale_part = (jnp.sum(row_max[:, 0:1] * row_dot[:, 0:1]) + jnp.sum(fc * col_dot) - diag) / batch
    col_sum = jnp.sum(jnp.where(lane_n < R, cl, 0.0))
    loss_part = (row_sum + col_sum - 2.0 * diag) / (2.0 * batch)
    sub8 = lax.broadcasted_iota(jnp.int32, (8, 128), 0)
    pst[me_p] = jnp.where(sub8 == 0, loss_part, jnp.where(sub8 == 1, scale_part, 0.0))
    plane = [send(pst.at[me_p], pst.at[me_p], o) for o in PLANE]

    transpose(0, NL // 2)
    text_product(6, 10)
    for dz in (2, 6):
        core_send(dz)
    image_product(0, 5)
    for dz in (2, 6):
        core_add(dz)
    zstep(2, 0)
    zstep(2, 1)
    for h in (0, 1):
        gathered(h, 2)
        pquarter(h)
    zstep(2, 2)
    for h in (0, 1):
        unit(h, 0)
    text_product(0, 6)
    for dz in (1, 7, 0):
        core_send(dz)
    for c in plane:
        c.wait_recv()
    zst[me_r] = jnp.sum(pst[...], axis=0)
    ring = [send(zst.at[me_r], zst.at[me_r], o) for o in RING]
    for dz in (1, 7, 0):
        core_add(dz)
    zstep(1, 0)
    zstep(1, 1)
    for h in (0, 1):
        gathered(h, 3)
        gathered(h, 1)
        punit(h)
    zstep(1, 2)
    for c in ring:
        c.wait_recv()
    out_s[...] = jnp.sum(zst[...], axis=0)
    for h in (0, 1):
        gathered(h, 0)
    for j in (0, 1, 2):
        zstep(0, j)
    out_t[...] = scale * gt[0:R, :]
    for h in (0, 1):
        image_out(h)
    for c in copies:
        c.wait_send()


def finish(gi, gt, s, out_i, out_t, out_loss, out_scale):
    out_i[...] = gi[...]
    out_t[...] = gt[...]
    out_loss[0] = jnp.max(s[0:1, 0:1])
    out_scale[0] = jnp.max(s[1:2, 0:1])


def per_device(image, text, log_scale):
    R, E = image.shape
    N = 16 * R
    batch = 256 * R
    H, EH = R // 2, E // 2
    vm = pltpu.VMEM
    vspec = pl.BlockSpec(memory_space=pltpu.VMEM)
    sspec = pl.BlockSpec(memory_space=pltpu.SMEM)
    hspec = pl.BlockSpec(memory_space=pltpu.HBM)
    one = jax.ShapeDtypeStruct((1,), F32)
    grad = jax.ShapeDtypeStruct((R, E), F32)
    gi, gt, s = pl.pallas_call(
        functools.partial(kernel, R, E, float(batch)),
        out_shape=(grad, grad, jax.ShapeDtypeStruct((8, 128), F32)),
        in_specs=[hspec, hspec, hspec],
        out_specs=(vspec, vspec, vspec),
        scratch_shapes=[
            vm((16, R, E), F32), vm((16, R, E), F32),
            vm((N, E), BF16), vm((N, E), BF16), vm((N, E), BF16), vm((N, E), BF16),
            vm((N, N), F32), vm((N, N), F32), vm((N, N), F32), vm((N, N), BF16), vm((N, N), BF16), vm((N, N), BF16), vm((N, N), BF16),
            vm((N, E), F32), vm((N, E), F32),
            vm((2, 4, 2, H, EH), F32), vm((2, 4, 2, H, E), F32),
            vm((2, 2, H, EH), F32), vm((2, 2, H, E), F32),
            vm((8, R, E), F32), vm((8, R, E), F32),
            vm((N, 128), F32), vm((N, 128), F32), vm((N, 128), F32), vm((N, 128), F32),
            vm((16, 8, 128), F32), vm((16, 8, 128), F32), vm((16, 8, 128), F32), vm((16, 8, 128), F32),
            pltpu.SMEM((1,), F32), pltpu.SMEM((16,), jnp.int32), pltpu.SemaphoreType.DMA((3,)),
            pltpu.SemaphoreType.DMA((N_COPIES,)), pltpu.SemaphoreType.DMA((N_COPIES,)),
        ],
        compiler_params=pltpu.CompilerParams(collective_id=0, has_side_effects=True, vmem_limit_bytes=54 * 2**20),
        cost_estimate=pl.CostEstimate(flops=18 * N * N * E, bytes_accessed=16 * R * E, transcendentals=6 * N * N),
    )(image, text, log_scale)
    out_i, out_t, loss, scale_grad = pl.pallas_call(
        finish,
        out_shape=(grad, grad, one, one),
        in_specs=[vspec, vspec, vspec],
        out_specs=(vspec, vspec, sspec, sspec),
    )(gi, gt, s)
    return loss, out_i, out_t, scale_grad


def solution(mesh):
    return jax.shard_map(
        per_device,
        mesh=mesh,
        in_specs=(P(("row", "col"), None), P(("col", "row"), None), P()),
        out_specs=(P(), P(("row", "col"), None), P(("col", "row"), None), P()),
        check_vma=False,
    )
```

```python
import functools

import jax
import jax.numpy as jnp
from jax import lax
from jax.experimental import pallas as pl
from jax.experimental.pallas import tpu as pltpu
from jax.sharding import PartitionSpec as P

MESH = pl.DeviceIdType.MESH
F32 = jnp.float32
BF16 = jnp.bfloat16

NX, NZ = 4, 8
IMG = [(0, 0), (3, 0), (1, 0), (0, 3), (0, 1),
       (3, 3), (3, 1), (1, 3), (1, 1), (0, 2), (2, 0),
       (3, 2), (2, 3), (1, 2), (2, 1), (2, 2)]
TXT = [(dz, dk) for dz in (0, 7, 1, 6, 2, 5, 3, 4) for dk in (0, 1)]
ISLOT = {p: i for i, p in enumerate(IMG)}
TSLOT = {p: i for i, p in enumerate(TXT)}
PLANE = [(x, y, 0, 0) for x in (2, 3, 1, 0) for y in (2, 3, 1, 0) if (x, y) != (0, 0)]
RING = [(0, 0, z, k) for z in (4, 3, 5, 2, 6, 1, 7, 0) for k in (1, 0) if (z, k) != (0, 0)]
NEXT = [(1, 0, 0, 0), (3, 0, 0, 0), (0, 1, 0, 0), (0, 3, 0, 0), (0, 0, 1, 0), (0, 0, 7, 0), (0, 0, 0, 1)]
N_COPIES = 208
CHUNK = {0: (0, 16), 1: (16, 16), 2: (32, 16), "p": (16, 8), "m": (24, 8)}


def position():
    r, c = lax.axis_index("row"), lax.axis_index("col")
    return c // 4, r // 4, ((r // 2) % 2) * 4 + c % 4, r % 2


def shard_of(image, x, y, z, k):
    row, col = (y * 2 + z // 4) * 2 + k, x * 4 + z % 4
    return row * 16 + col if image else col * 16 + row


def split(v):
    hi = v.astype(BF16)
    return hi, (v - hi.astype(F32)).astype(BF16)


def dot3(ah, al, bh, bl, dims):
    d = functools.partial(lax.dot_general, dimension_numbers=(dims, ((), ())), preferred_element_type=F32)
    return d(ah, bh) + (d(al, bh) + d(ah, bl))


def kernel(R, E, batch, im, tx, ls_hbm, out_i, out_t, out_s,
           img, txt, ih, il, th, tl, lg, er, ec, wh, wl, wth, wtl, gi, gt,
           rq, ru, rpq, rpu, rz, rc, cols_a, cols_b, row_max, row_dot, rst, cst, pst, zst, ls, rid, lsem, ssem, rsem):
    H = R // 2
    EH = E // 2
    N = 16 * R
    x, y, z, k = position()

    def peer(o):
        px, py, pz, pk = (x + o[0]) % 4, (y + o[1]) % 4, (z + o[2]) % 8, (k + o[3]) % 2
        return ((py * 2 + pz // 4) * 2 + pk, px * 4 + pz % 4)

    copies = []

    def send(src, dst, o):
        i = len(copies)
        c = pltpu.make_async_remote_copy(src_ref=src, dst_ref=dst, send_sem=ssem.at[i], recv_sem=rsem.at[i],
                                         device_id=peer(o), device_id_type=MESH)
        c.start()
        copies.append(c)
        return c

    CORE = (0, 0, 0, 1)

    def zdir(s):
        return (0, 0, s % 8, 0)

    def idir(h, primary, s):
        return (s % 4, 0, 0, 0) if (h == 0) == primary else (0, s % 4, 0, 0)

    def pos(h, p, q):
        p, q = p % 4, q % 4
        return (p, q) if h == 0 else (q, p)

    HALF = {"f": pl.ds(0, E), "A": pl.ds(0, EH), "B": pl.ds(EH, EH)}

    barrier = pltpu.get_barrier_semaphore()
    for o in NEXT:
        pl.semaphore_signal(barrier, inc=1, device_id=peer(o), device_id_type=MESH)
    local = [pltpu.make_async_copy(im, img.at[0], lsem.at[0]), pltpu.make_async_copy(tx, txt.at[0], lsem.at[1]),
             pltpu.make_async_copy(ls_hbm, ls, lsem.at[2])]
    for c in local:
        c.start()
    for s, (dx, dy) in enumerate(IMG):
        rid[s] = shard_of(True, (x + dx) % 4, (y + dy) % 4, z, k) * R
    for c in local:
        c.wait()
    pl.semaphore_wait(barrier, len(NEXT))

    got = {}

    def isend(h, p, q, primary, s, part="f"):
        o = pos(h, p, q)
        rows = pl.ds(h * H, H)
        src = img.at[ISLOT[o], rows, HALF[part]]
        to = pos(h, p - s, q) if primary else pos(h, p, q - s)
        got[("i", h, to, part)] = send(src, img.at[ISLOT[to], rows, HALF[part]], idir(h, primary, s))

    def iwait(h, p, q):
        o = pos(h, p, q)
        for part in ("f", "A", "B"):
            c = got.pop(("i", h, o, part), None)
            if c is not None:
                c.wait_recv()

    def tsend(dz, s, ch):
        rows = pl.ds(*CHUNK[ch])
        to = (dz - s) % 8
        got[("t", to, ch)] = send(txt.at[TSLOT[(dz, 0)], rows, :], txt.at[TSLOT[(to, 0)], rows, :], zdir(s))

    def tpass(d, ch):
        for dz, s in ((8 - d, 1), (d, -1)):
            got.pop(("t", dz, ch)).wait_recv()
            nxt = ch if d < 3 else {(1, 0): 0, (1, 1): "p", (-1, 1): "m", (-1, 2): 2}.get((s, ch))
            if nxt is not None:
                tsend(dz, s, nxt)

    def tlast():
        for ch in (0, "p", "m", 2):
            got.pop(("t", 4, ch)).wait_recv()

    def tlast_core():
        for ch in (0, 2, "p", "m"):
            got.pop(("t", 4, ch)).wait_recv()
            rows = pl.ds(*CHUNK[ch])
            got[("c4", ch)] = send(txt.at[TSLOT[(4, 0)], rows, :], txt.at[TSLOT[(4, 1)], rows, :], CORE)

    def cwait4():
        for ch in (0, 2, "p", "m"):
            got.pop(("c4", ch)).wait_recv()

    def tcore(dz):
        got[("c", dz)] = send(txt.at[TSLOT[(dz, 0)]], txt.at[TSLOT[(dz, 1)]], CORE)

    def cwait(dz):
        got.pop(("c", dz)).wait_recv()

    def put(hi_ref, lo_ref, s, v):
        rows = pl.ds(s * R if isinstance(s, int) else pl.multiple_of(s * R, R), R)
        hi_ref[rows, :], lo_ref[rows, :] = split(v)

    def conv(ref, hi_ref, lo_ref, a, b):
        def body(s, _):
            put(hi_ref, lo_ref, s, ref[s])
            return 0
        lax.fori_loop(a, b, body, 0)

    scale = jnp.exp(jnp.full((1, 1), ls[0], F32))

    def logits(a, b, t0, t1):
        rows = slice(a * R, b * R)

        def body(t, _):
            cs = pl.ds(pl.multiple_of(t * 256, 256), 256)
            lg[rows, cs] = scale * dot3(ih[rows, :], il[rows, :], th[cs, :], tl[cs, :], ((1,), (1,)))
            return 0
        lax.fori_loop(t0, t1, body, 0)

    def ipass(h, p, q, primary, s):
        isend(h, p, q, primary, s, "A" if s == 1 else "B")

    def second(p):
        for h in (0, 1):
            iwait(h, p, 3)
            ipass(h, p, 3, False, 1)
            iwait(h, p, 1)
            ipass(h, p, 1, False, -1)

    def third(p):
        for h in (0, 1):
            iwait(h, p, 2)

    for h in (0, 1):
        isend(h, 0, 0, True, 1)
        isend(h, 0, 0, True, -1)
    for ch in (0, 1, 2):
        tsend(0, 1, ch)
        tsend(0, -1, ch)
    for h in (0, 1):
        isend(h, 0, 0, False, 1)
        isend(h, 0, 0, False, -1)
    tcore(0)
    put(ih, il, 0, img[0])
    put(th, tl, 0, txt[0])

    tpass(1, 0)
    for h in (0, 1):
        iwait(h, 3, 0)
        ipass(h, 3, 0, True, 1)
        iwait(h, 1, 0)
        ipass(h, 1, 0, True, -1)
    for p in (3, 1):
        for h in (0, 1):
            isend(h, p, 0, False, 1)
            isend(h, p, 0, False, -1)
    tpass(1, 1)
    second(0)
    tpass(1, 2)
    tcore(7)
    tcore(1)
    for h in (0, 1):
        iwait(h, 2, 0)
        isend(h, 2, 0, False, 1)
        isend(h, 2, 0, False, -1)
    conv(img, ih, il, 1, 5)
    tpass(2, 0)
    for dz in (0, 7, 1):
        cwait(dz)
    conv(txt, th, tl, 1, 6)
    tpass(2, 1)
    logits(0, 5, 0, 1)
    second(3)
    tpass(2, 2)
    tcore(6)
    tcore(2)
    second(1)
    tpass(3, 0)
    cwait(6)
    cwait(2)
    conv(img, ih, il, 5, 9)
    third(0)
    tpass(3, 1)
    conv(txt, th, tl, 6, 10)
    second(2)
    tpass(3, 2)
    tcore(5)
    tcore(3)
    conv(img, ih, il, 9, 11)
    logits(5, 11, 0, 1)
    third(3)
    cwait(5)
    cwait(3)
    conv(txt, th, tl, 10, 14)
    logits(0, 11, 1, 2)
    tlast_core()
    third(1)
    conv(img, ih, il, 11, 15)
    logits(11, 15, 0, 2)
    cwait4()
    conv(txt, th, tl, 14, 16)
    logits(0, 15, 2, 3)
    third(2)
    conv(img, ih, il, 15, 16)
    logits(15, 16, 0, 3)

    RB = 2 * R
    NB = N // RB

    def rows_body(i, cm):
        rows = pl.ds(pl.multiple_of(i * RB, RB), RB)
        v = lg[rows, :]
        rm = jnp.max(v, axis=1, keepdims=True)
        e = jnp.exp(v - rm)
        er[rows, :] = e
        row_max[rows, :] = jnp.broadcast_to(rm, (RB, 128))
        rl = rm + jnp.log(jnp.sum(e, axis=1, keepdims=True))
        cols_a[rows, :] = jnp.broadcast_to(rl, (RB, 128))
        return jnp.maximum(cm, jnp.max(v.reshape(RB // 8, 8, N), axis=0))

    cm = lax.fori_loop(0, NB, rows_body, jnp.full((8, N), -jnp.inf, F32))
    cm = jnp.max(cm, axis=0, keepdims=True)

    def cols_body(i, cs):
        rows = pl.ds(pl.multiple_of(i * RB, RB), RB)
        e = jnp.exp(lg[rows, :] - cm)
        ec[rows, :] = e
        return cs + jnp.sum(e.reshape(RB // 8, 8, N), axis=0)

    NL = N // 128
    lane = lax.broadcasted_iota(jnp.int32, (128, 128), 1)

    def to_rows(ref):
        m = jnp.zeros((128, 128), F32)
        for b in range(NL):
            m = jnp.where(lane == b, ref[b * 128:(b + 1) * 128, :], m)
        return m.T[:8, :]

    def to_cols(ref, v):
        m = jnp.concatenate([v, jnp.zeros((120, 128), F32)], axis=0).T
        for b in range(NL):
            ref[b * 128:(b + 1) * 128, :] = jnp.broadcast_to(m[:, b:b + 1], (128, 128))

    def iabs(s):
        return ((x + IMG[s][0]) % 4) * 4 + (y + IMG[s][1]) % 4

    def tabs(s):
        return ((z + TXT[s][0]) % 8) * 2 + (k + TXT[s][1]) % 2

    def to_abs(where):
        for s in range(16):
            cols_b[pl.ds(pl.multiple_of(where(s) * R, R), R), :] = cols_a[s * R:(s + 1) * R, :]

    def to_rel(where):
        for s in range(16):
            cols_a[s * R:(s + 1) * R, :] = cols_b[pl.ds(pl.multiple_of(where(s) * R, R), R), :]

    me_p, me_r = x * 4 + y, z * 2 + k
    to_abs(iabs)
    rst[me_p] = to_rows(cols_b)
    plane = [send(rst.at[me_p], rst.at[me_p], o) for o in PLANE]
    cs = lax.fori_loop(0, NB, cols_body, jnp.zeros((8, N), F32))
    cl = cm + jnp.log(jnp.sum(cs, axis=0, keepdims=True))
    c8 = jnp.concatenate([cl[:, b * 128:(b + 1) * 128] for b in range(NL)] + [jnp.zeros((8 - NL, 128), F32)], axis=0)
    to_cols(cols_a, c8)
    to_abs(tabs)
    cst[me_r] = to_rows(cols_b)
    ring = [send(cst.at[me_r], cst.at[me_r], o) for o in RING]

    def merge(ref):
        v = ref[...]
        m = jnp.max(v, axis=0)
        return m + jnp.log(jnp.sum(jnp.exp(v - m[None]), axis=0))

    lane_n = lax.broadcasted_iota(jnp.int32, (1, N), 1)
    cid = lane_n
    for s, (dz, dk) in enumerate(TXT):
        base = shard_of(False, x, y, (z + dz) % 8, (k + dk) % 2) * R - s * R
        cid = jnp.where((lane_n >= s * R) & (lane_n < (s + 1) * R), lane_n + base, cid)

    sub = lax.broadcasted_iota(jnp.int32, (R, N), 0)

    def tile_rows(s):
        rows = pl.ds(pl.multiple_of(s * R, R), R)
        return rows, (cid - rid[s]) == sub

    def dots_body(s, c):
        rows, hit = tile_rows(s)
        v = lg[rows, :]
        a, d = c
        row_dot[rows, :] = jnp.broadcast_to(jnp.sum(er[rows, :] * v, axis=1, keepdims=True), (R, 128))
        a = a + jnp.sum((ec[rows, :] * v).reshape(R // 8, 8, N), axis=0)
        d = d + jnp.sum(jnp.where(hit, v, 0.0).reshape(R // 8, 8, N), axis=0)
        return a, d

    zero = jnp.zeros((8, N), F32)
    col_dot, diag = lax.fori_loop(0, 16, dots_body, (zero, zero))
    col_dot = jnp.sum(col_dot, axis=0, keepdims=True)
    diag = jnp.sum(diag)

    for c in plane:
        c.wait_recv()
    to_cols(cols_b, merge(rst))
    to_rel(iabs)
    row_sum = jnp.sum(cols_a[0:R, 0:1])
    row_max[...] = 0.5 * jnp.exp(row_max[...] - cols_a[...])
    for c in ring:
        c.wait_recv()
    to_cols(cols_b, merge(cst))
    to_rel(tabs)
    c8 = to_rows(cols_a)
    cl = jnp.concatenate([c8[b:b + 1, :] for b in range(NL)], axis=1)
    fc = 0.5 * jnp.exp(cm - cl)

    def weights_body(s, _):
        rows, hit = tile_rows(s)
        w = er[rows, :] * row_max[rows, 0:1] + ec[rows, :] * fc
        wh[rows, :], wl[rows, :] = split(jnp.where(hit, w - 1.0, w))
        return 0

    lax.fori_loop(0, 16, weights_body, 0)

    def transpose(b0, b1):
        def body(b, _):
            cs = pl.ds(pl.multiple_of(b * 128, 128), 128)
            wth[cs, :] = wh[:, cs].T
            wtl[cs, :] = wl[:, cs].T
            return 0
        lax.fori_loop(b0, b1, body, 0)

    def product(dst, ah, al, bh, bl, a, b):
        rows = slice(a * R, b * R)

        def body(n, _):
            cs = pl.ds(pl.multiple_of(n * (E // 2), 128), E // 2)
            dst[rows, cs] = dot3(ah[rows, :], al[rows, :], bh[:, cs], bl[:, cs], ((1,), (0,)))
            return 0
        lax.fori_loop(0, 2, body, 0)

    def image_product(a, b):
        product(gi, wh, wl, th, tl, a, b)

    def text_product(a, b):
        product(gt, wth, wtl, ih, il, a, b)

    COL = {"f": slice(0, E), "A": slice(0, EH), "B": slice(EH, E)}
    red = {}

    def grows(h, o):
        return ISLOT[o] * R + h * H

    def quarter(h, p):
        o = pos(h, p, 2)
        r = pl.ds(grows(h, o), H)
        red[("q", h, p, 1)] = send(gi.at[r, HALF["A"]], rq.at[h, p, 0], idir(h, False, 1))
        red[("q", h, p, 3)] = send(gi.at[r, HALF["B"]], rq.at[h, p, 1], idir(h, False, -1))

    def unit(h, p):
        for q, part, j, s in ((1, "A", 0, 1), (3, "B", 1, -1)):
            red.pop(("q", h, p, q)).wait_recv()
            a = grows(h, pos(h, p, q))
            gi[a:a + H, COL[part]] += rq[h, p, j]
            red[("u", h, p, q)] = send(gi.at[pl.ds(a, H), :], ru.at[h, p, j], idir(h, False, s))

    def gathered(h, p):
        a = grows(h, pos(h, p, 0))
        for q in (1, 3):
            red.pop(("u", h, p, q)).wait_recv()
        gi[a:a + H, :] += ru[h, p, 0] + ru[h, p, 1]

    def pquarter(h):
        r = pl.ds(grows(h, pos(h, 2, 0)), H)
        red[("pq", h, 1)] = send(gi.at[r, HALF["A"]], rpq.at[h, 0], idir(h, True, 1))
        red[("pq", h, 3)] = send(gi.at[r, HALF["B"]], rpq.at[h, 1], idir(h, True, -1))

    def punit(h):
        for p, part, j, s in ((1, "A", 0, 1), (3, "B", 1, -1)):
            red.pop(("pq", h, p)).wait_recv()
            a = grows(h, pos(h, p, 0))
            gi[a:a + H, COL[part]] += rpq[h, j]
            red[("pu", h, p)] = send(gi.at[pl.ds(a, H), :], rpu.at[h, j], idir(h, True, s))

    def image_out(h):
        for p in (1, 3):
            red.pop(("pu", h, p)).wait_recv()
        a = grows(h, (0, 0))
        out_i[h * H:(h + 1) * H, :] = scale * (gi[a:a + H, :] + (rpu[h, 0] + rpu[h, 1]))

    def core_send(dz):
        red[("c", dz)] = send(gt.at[pl.ds(TSLOT[(dz, 1)] * R, R), :], rc.at[dz], CORE)

    def core_add(dz):
        red.pop(("c", dz)).wait_recv()
        a = TSLOT[(dz, 0)] * R
        gt[a:a + R, :] += rc[dz]

    def zsend(dz, s, ch):
        a, n = CHUNK[ch]
        src = gt.at[pl.ds(TSLOT[(dz, 0)] * R + a, n), :]
        red[("z", (dz - s) % 8, s, ch)] = send(src, rz.at[dz, pl.ds(a, n), :], zdir(s))

    def zadd(dz, s, ch):
        red.pop(("z", dz, s, ch)).wait_recv()
        a, n = CHUNK[ch]
        g = TSLOT[(dz, 0)] * R + a
        gt[g:g + n, :] += rz[(dz + s) % 8, a:a + n, :]

    def zstep(d, j):
        for dz, s, ch in ((d, 1, (2, 0, 1)[j]), (8 - d, -1, (0, 2, 1)[j])):
            if d == 3:
                came = None if j == 0 else ch if j == 1 else ("p" if s == 1 else "m")
            else:
                came = ch
            if came is not None:
                zadd(dz % 8, s, came)
            if d > 0:
                zsend(dz, s, ch)

    transpose(NL - 1, NL)
    text_product(14, 16)
    core_send(4)
    image_product(11, 16)
    for p in (2, 3, 1):
        for h in (0, 1):
            quarter(h, p)
    core_add(4)
    for s, ch in ((1, 0), (-1, 2), (1, "p"), (-1, "m")):
        zsend(4, s, ch)
    transpose(NL // 2, NL - 1)
    text_product(10, 14)
    for dz in (3, 5):
        core_send(dz)
    for h in (0, 1):
        unit(h, 2)
    for dz in (3, 5):
        core_add(dz)
    zstep(3, 0)
    image_product(5, 11)
    for h in (0, 1):
        quarter(h, 0)
    zstep(3, 1)
    for p in (3, 1):
        for h in (0, 1):
            unit(h, p)
    zstep(3, 2)

    scale_part = (jnp.sum(row_max[:, 0:1] * row_dot[:, 0:1]) + jnp.sum(fc * col_dot) - diag) / batch
    col_sum = jnp.sum(jnp.where(lane_n < R, cl, 0.0))
    loss_part = (row_sum + col_sum - 2.0 * diag) / (2.0 * batch)
    sub8 = lax.broadcasted_iota(jnp.int32, (8, 128), 0)
    pst[me_p] = jnp.where(sub8 == 0, loss_part, jnp.where(sub8 == 1, scale_part, 0.0))
    plane = [send(pst.at[me_p], pst.at[me_p], o) for o in PLANE]

    transpose(0, NL // 2)
    text_product(6, 10)
    for dz in (2, 6):
        core_send(dz)
    image_product(0, 5)
    for dz in (2, 6):
        core_add(dz)
    zstep(2, 0)
    zstep(2, 1)
    for h in (0, 1):
        gathered(h, 2)
        pquarter(h)
    zstep(2, 2)
    for h in (0, 1):
        unit(h, 0)
    text_product(0, 6)
    for dz in (1, 7, 0):
        core_send(dz)
    for c in plane:
        c.wait_recv()
    zst[me_r] = jnp.sum(pst[...], axis=0)
    ring = [send(zst.at[me_r], zst.at[me_r], o) for o in RING]
    for dz in (1, 7, 0):
        core_add(dz)
    zstep(1, 0)
    zstep(1, 1)
    for h in (0, 1):
        gathered(h, 3)
        gathered(h, 1)
        punit(h)
    zstep(1, 2)
    for c in ring:
        c.wait_recv()
    out_s[...] = jnp.sum(zst[...], axis=0)
    for h in (0, 1):
        gathered(h, 0)
    for j in (0, 1, 2):
        zstep(0, j)
    out_t[...] = scale * gt[0:R, :]
    for h in (0, 1):
        image_out(h)
    for c in copies:
        c.wait_send()


def finish(gi, gt, s, out_i, out_t, out_loss, out_scale):
    out_i[...] = gi[...]
    out_t[...] = gt[...]
    out_loss[0] = jnp.max(s[0:1, 0:1])
    out_scale[0] = jnp.max(s[1:2, 0:1])


def per_device(image, text, log_scale):
    R, E = image.shape
    N = 16 * R
    batch = 256 * R
    H, EH = R // 2, E // 2
    vm = pltpu.VMEM
    vspec = pl.BlockSpec(memory_space=pltpu.VMEM)
    sspec = pl.BlockSpec(memory_space=pltpu.SMEM)
    hspec = pl.BlockSpec(memory_space=pltpu.HBM)
    one = jax.ShapeDtypeStruct((1,), F32)
    grad = jax.ShapeDtypeStruct((R, E), F32)
    gi, gt, s = pl.pallas_call(
        functools.partial(kernel, R, E, float(batch)),
        out_shape=(grad, grad, jax.ShapeDtypeStruct((8, 128), F32)),
        in_specs=[hspec, hspec, hspec],
        out_specs=(vspec, vspec, vspec),
        scratch_shapes=[
            vm((16, R, E), F32), vm((16, R, E), F32),
            vm((N, E), BF16), vm((N, E), BF16), vm((N, E), BF16), vm((N, E), BF16),
            vm((N, N), F32), vm((N, N), F32), vm((N, N), F32), vm((N, N), BF16), vm((N, N), BF16), vm((N, N), BF16), vm((N, N), BF16),
            vm((N, E), F32), vm((N, E), F32),
            vm((2, 4, 2, H, EH), F32), vm((2, 4, 2, H, E), F32),
            vm((2, 2, H, EH), F32), vm((2, 2, H, E), F32),
            vm((8, R, E), F32), vm((8, R, E), F32),
            vm((N, 128), F32), vm((N, 128), F32), vm((N, 128), F32), vm((N, 128), F32),
            vm((16, 8, 128), F32), vm((16, 8, 128), F32), vm((16, 8, 128), F32), vm((16, 8, 128), F32),
            pltpu.SMEM((1,), F32), pltpu.SMEM((16,), jnp.int32), pltpu.SemaphoreType.DMA((3,)),
            pltpu.SemaphoreType.DMA((N_COPIES,)), pltpu.SemaphoreType.DMA((N_COPIES,)),
        ],
        compiler_params=pltpu.CompilerParams(collective_id=0, has_side_effects=True, vmem_limit_bytes=54 * 2**20),
        cost_estimate=pl.CostEstimate(flops=18 * N * N * E, bytes_accessed=16 * R * E, transcendentals=6 * N * N),
    )(image, text, log_scale)
    out_i, out_t, loss, scale_grad = pl.pallas_call(
        finish,
        out_shape=(grad, grad, one, one),
        in_specs=[vspec, vspec, vspec],
        out_specs=(vspec, vspec, sspec, sspec),
    )(gi, gt, s)
    return loss, out_i, out_t, scale_grad


def solution(mesh):
    return jax.shard_map(
        per_device,
        mesh=mesh,
        in_specs=(P(("row", "col"), None), P(("col", "row"), None), P()),
        out_specs=(P(), P(("row", "col"), None), P(("col", "row"), None), P()),
        check_vma=False,
    )
```

```python
import functools

import jax
import jax.numpy as jnp
from jax import lax
from jax.experimental import pallas as pl
from jax.experimental.pallas import tpu as pltpu
from jax.sharding import PartitionSpec as P

MESH = pl.DeviceIdType.MESH
F32 = jnp.float32
BF16 = jnp.bfloat16

NX, NZ = 4, 8
IMG = [(0, 0), (3, 0), (1, 0), (0, 3), (0, 1),
       (3, 3), (3, 1), (1, 3), (1, 1), (0, 2), (2, 0),
       (3, 2), (2, 3), (1, 2), (2, 1), (2, 2)]
TXT = [(dz, dk) for dz in (0, 7, 1, 6, 2, 5, 3, 4) for dk in (0, 1)]
ISLOT = {p: i for i, p in enumerate(IMG)}
TSLOT = {p: i for i, p in enumerate(TXT)}
PLANE = [(x, y, 0, 0) for x in (2, 3, 1, 0) for y in (2, 3, 1, 0) if (x, y) != (0, 0)]
RING = [(0, 0, z, k) for z in (4, 3, 5, 2, 6, 1, 7, 0) for k in (1, 0) if (z, k) != (0, 0)]
NEXT = [(1, 0, 0, 0), (3, 0, 0, 0), (0, 1, 0, 0), (0, 3, 0, 0), (0, 0, 1, 0), (0, 0, 7, 0), (0, 0, 0, 1)]
N_COPIES = 208
CHUNK = {0: (0, 16), 1: (16, 16), 2: (32, 16), "p": (16, 8), "m": (24, 8)}


def position():
    r, c = lax.axis_index("row"), lax.axis_index("col")
    return c // 4, r // 4, ((r // 2) % 2) * 4 + c % 4, r % 2


def shard_of(image, x, y, z, k):
    row, col = (y * 2 + z // 4) * 2 + k, x * 4 + z % 4
    return row * 16 + col if image else col * 16 + row


def split(v):
    hi = v.astype(BF16)
    return hi, (v - hi.astype(F32)).astype(BF16)


def dot3(ah, al, bh, bl, dims):
    d = functools.partial(lax.dot_general, dimension_numbers=(dims, ((), ())), preferred_element_type=F32)
    m = ah.shape[0]
    t = d(jnp.concatenate([ah, al], axis=0), bh)
    return t[:m] + (t[m:] + d(ah, bl))


def kernel(R, E, batch, im, tx, ls_hbm, out_i, out_t, out_s,
           img, txt, ih, il, th, tl, lg, er, ec, wh, wl, wth, wtl, gi, gt,
           rq, ru, rpq, rpu, rz, rc, cols_a, cols_b, row_max, row_dot, rst, cst, pst, zst, ls, rid, lsem, ssem, rsem):
    H = R // 2
    EH = E // 2
    N = 16 * R
    x, y, z, k = position()

    def peer(o):
        px, py, pz, pk = (x + o[0]) % 4, (y + o[1]) % 4, (z + o[2]) % 8, (k + o[3]) % 2
        return ((py * 2 + pz // 4) * 2 + pk, px * 4 + pz % 4)

    copies = []

    def send(src, dst, o):
        i = len(copies)
        c = pltpu.make_async_remote_copy(src_ref=src, dst_ref=dst, send_sem=ssem.at[i], recv_sem=rsem.at[i],
                                         device_id=peer(o), device_id_type=MESH)
        c.start()
        copies.append(c)
        return c

    CORE = (0, 0, 0, 1)

    def zdir(s):
        return (0, 0, s % 8, 0)

    def idir(h, primary, s):
        return (s % 4, 0, 0, 0) if (h == 0) == primary else (0, s % 4, 0, 0)

    def pos(h, p, q):
        p, q = p % 4, q % 4
        return (p, q) if h == 0 else (q, p)

    HALF = {"f": pl.ds(0, E), "A": pl.ds(0, EH), "B": pl.ds(EH, EH)}

    barrier = pltpu.get_barrier_semaphore()
    for o in NEXT:
        pl.semaphore_signal(barrier, inc=1, device_id=peer(o), device_id_type=MESH)
    local = [pltpu.make_async_copy(im, img.at[0], lsem.at[0]), pltpu.make_async_copy(tx, txt.at[0], lsem.at[1]),
             pltpu.make_async_copy(ls_hbm, ls, lsem.at[2])]
    for c in local:
        c.start()
    for s, (dx, dy) in enumerate(IMG):
        rid[s] = shard_of(True, (x + dx) % 4, (y + dy) % 4, z, k) * R
    for c in local:
        c.wait()
    pl.semaphore_wait(barrier, len(NEXT))

    got = {}

    def isend(h, p, q, primary, s, part="f"):
        o = pos(h, p, q)
        rows = pl.ds(h * H, H)
        src = img.at[ISLOT[o], rows, HALF[part]]
        to = pos(h, p - s, q) if primary else pos(h, p, q - s)
        got[("i", h, to, part)] = send(src, img.at[ISLOT[to], rows, HALF[part]], idir(h, primary, s))

    def iwait(h, p, q):
        o = pos(h, p, q)
        for part in ("f", "A", "B"):
            c = got.pop(("i", h, o, part), None)
            if c is not None:
                c.wait_recv()

    def tsend(dz, s, ch):
        rows = pl.ds(*CHUNK[ch])
        to = (dz - s) % 8
        got[("t", to, ch)] = send(txt.at[TSLOT[(dz, 0)], rows, :], txt.at[TSLOT[(to, 0)], rows, :], zdir(s))

    def tpass(d, ch):
        for dz, s in ((8 - d, 1), (d, -1)):
            got.pop(("t", dz, ch)).wait_recv()
            nxt = ch if d < 3 else {(1, 0): 0, (1, 1): "p", (-1, 1): "m", (-1, 2): 2}.get((s, ch))
            if nxt is not None:
                tsend(dz, s, nxt)

    def tlast():
        for ch in (0, "p", "m", 2):
            got.pop(("t", 4, ch)).wait_recv()

    def tlast_core():
        for ch in (0, 2, "p", "m"):
            got.pop(("t", 4, ch)).wait_recv()
            rows = pl.ds(*CHUNK[ch])
            got[("c4", ch)] = send(txt.at[TSLOT[(4, 0)], rows, :], txt.at[TSLOT[(4, 1)], rows, :], CORE)

    def cwait4():
        for ch in (0, 2, "p", "m"):
            got.pop(("c4", ch)).wait_recv()

    def tcore(dz):
        got[("c", dz)] = send(txt.at[TSLOT[(dz, 0)]], txt.at[TSLOT[(dz, 1)]], CORE)

    def cwait(dz):
        got.pop(("c", dz)).wait_recv()

    def put(hi_ref, lo_ref, s, v):
        rows = pl.ds(s * R if isinstance(s, int) else pl.multiple_of(s * R, R), R)
        hi_ref[rows, :], lo_ref[rows, :] = split(v)

    def conv(ref, hi_ref, lo_ref, a, b):
        def body(s, _):
            put(hi_ref, lo_ref, s, ref[s])
            return 0
        lax.fori_loop(a, b, body, 0)

    scale = jnp.exp(jnp.full((1, 1), ls[0], F32))

    def logits(a, b, t0, t1):
        rows = slice(a * R, b * R)

        def body(t, _):
            cs = pl.ds(pl.multiple_of(t * 256, 256), 256)
            lg[rows, cs] = scale * dot3(ih[rows, :], il[rows, :], th[cs, :], tl[cs, :], ((1,), (1,)))
            return 0
        lax.fori_loop(t0, t1, body, 0)

    def ipass(h, p, q, primary, s):
        isend(h, p, q, primary, s, "A" if s == 1 else "B")

    def second(p):
        for h in (0, 1):
            iwait(h, p, 3)
            ipass(h, p, 3, False, 1)
            iwait(h, p, 1)
            ipass(h, p, 1, False, -1)

    def third(p):
        for h in (0, 1):
            iwait(h, p, 2)

    for h in (0, 1):
        isend(h, 0, 0, True, 1)
        isend(h, 0, 0, True, -1)
    for ch in (0, 1, 2):
        tsend(0, 1, ch)
        tsend(0, -1, ch)
    for h in (0, 1):
        isend(h, 0, 0, False, 1)
        isend(h, 0, 0, False, -1)
    tcore(0)
    put(ih, il, 0, img[0])
    put(th, tl, 0, txt[0])

    tpass(1, 0)
    for h in (0, 1):
        iwait(h, 3, 0)
        ipass(h, 3, 0, True, 1)
        iwait(h, 1, 0)
        ipass(h, 1, 0, True, -1)
    for p in (3, 1):
        for h in (0, 1):
            isend(h, p, 0, False, 1)
            isend(h, p, 0, False, -1)
    tpass(1, 1)
    second(0)
    tpass(1, 2)
    tcore(7)
    tcore(1)
    for h in (0, 1):
        iwait(h, 2, 0)
        isend(h, 2, 0, False, 1)
        isend(h, 2, 0, False, -1)
    conv(img, ih, il, 1, 5)
    tpass(2, 0)
    for dz in (0, 7, 1):
        cwait(dz)
    conv(txt, th, tl, 1, 6)
    tpass(2, 1)
    logits(0, 5, 0, 1)
    second(3)
    tpass(2, 2)
    tcore(6)
    tcore(2)
    second(1)
    tpass(3, 0)
    cwait(6)
    cwait(2)
    conv(img, ih, il, 5, 9)
    third(0)
    tpass(3, 1)
    conv(txt, th, tl, 6, 10)
    second(2)
    tpass(3, 2)
    tcore(5)
    tcore(3)
    conv(img, ih, il, 9, 11)
    logits(5, 11, 0, 1)
    third(3)
    cwait(5)
    cwait(3)
    conv(txt, th, tl, 10, 14)
    logits(0, 11, 1, 2)
    tlast_core()
    third(1)
    conv(img, ih, il, 11, 15)
    logits(11, 15, 0, 2)
    cwait4()
    conv(txt, th, tl, 14, 16)
    logits(0, 15, 2, 3)
    third(2)
    conv(img, ih, il, 15, 16)
    logits(15, 16, 0, 3)

    RB = 2 * R
    NB = N // RB

    def rows_body(i, cm):
        rows = pl.ds(pl.multiple_of(i * RB, RB), RB)
        v = lg[rows, :]
        rm = jnp.max(v, axis=1, keepdims=True)
        e = jnp.exp(v - rm)
        er[rows, :] = e
        row_max[rows, :] = jnp.broadcast_to(rm, (RB, 128))
        rl = rm + jnp.log(jnp.sum(e, axis=1, keepdims=True))
        cols_a[rows, :] = jnp.broadcast_to(rl, (RB, 128))
        return jnp.maximum(cm, jnp.max(v.reshape(RB // 8, 8, N), axis=0))

    cm = lax.fori_loop(0, NB, rows_body, jnp.full((8, N), -jnp.inf, F32))
    cm = jnp.max(cm, axis=0, keepdims=True)

    def cols_body(i, cs):
        rows = pl.ds(pl.multiple_of(i * RB, RB), RB)
        e = jnp.exp(lg[rows, :] - cm)
        ec[rows, :] = e
        return cs + jnp.sum(e.reshape(RB // 8, 8, N), axis=0)

    NL = N // 128
    lane = lax.broadcasted_iota(jnp.int32, (128, 128), 1)

    def to_rows(ref):
        m = jnp.zeros((128, 128), F32)
        for b in range(NL):
            m = jnp.where(lane == b, ref[b * 128:(b + 1) * 128, :], m)
        return m.T[:8, :]

    def to_cols(ref, v):
        m = jnp.concatenate([v, jnp.zeros((120, 128), F32)], axis=0).T
        for b in range(NL):
            ref[b * 128:(b + 1) * 128, :] = jnp.broadcast_to(m[:, b:b + 1], (128, 128))

    def iabs(s):
        return ((x + IMG[s][0]) % 4) * 4 + (y + IMG[s][1]) % 4

    def tabs(s):
        return ((z + TXT[s][0]) % 8) * 2 + (k + TXT[s][1]) % 2

    def to_abs(where):
        for s in range(16):
            cols_b[pl.ds(pl.multiple_of(where(s) * R, R), R), :] = cols_a[s * R:(s + 1) * R, :]

    def to_rel(where):
        for s in range(16):
            cols_a[s * R:(s + 1) * R, :] = cols_b[pl.ds(pl.multiple_of(where(s) * R, R), R), :]

    me_p, me_r = x * 4 + y, z * 2 + k
    to_abs(iabs)
    rst[me_p] = to_rows(cols_b)
    plane = [send(rst.at[me_p], rst.at[me_p], o) for o in PLANE]
    cs = lax.fori_loop(0, NB, cols_body, jnp.zeros((8, N), F32))
    cl = cm + jnp.log(jnp.sum(cs, axis=0, keepdims=True))
    c8 = jnp.concatenate([cl[:, b * 128:(b + 1) * 128] for b in range(NL)] + [jnp.zeros((8 - NL, 128), F32)], axis=0)
    to_cols(cols_a, c8)
    to_abs(tabs)
    cst[me_r] = to_rows(cols_b)
    ring = [send(cst.at[me_r], cst.at[me_r], o) for o in RING]

    def merge(ref):
        v = ref[...]
        m = jnp.max(v, axis=0)
        return m + jnp.log(jnp.sum(jnp.exp(v - m[None]), axis=0))

    lane_n = lax.broadcasted_iota(jnp.int32, (1, N), 1)
    cid = lane_n
    for s, (dz, dk) in enumerate(TXT):
        base = shard_of(False, x, y, (z + dz) % 8, (k + dk) % 2) * R - s * R
        cid = jnp.where((lane_n >= s * R) & (lane_n < (s + 1) * R), lane_n + base, cid)

    sub = lax.broadcasted_iota(jnp.int32, (R, N), 0)

    def tile_rows(s):
        rows = pl.ds(pl.multiple_of(s * R, R), R)
        return rows, (cid - rid[s]) == sub

    def dots_body(s, c):
        rows, hit = tile_rows(s)
        v = lg[rows, :]
        a, d = c
        row_dot[rows, :] = jnp.broadcast_to(jnp.sum(er[rows, :] * v, axis=1, keepdims=True), (R, 128))
        a = a + jnp.sum((ec[rows, :] * v).reshape(R // 8, 8, N), axis=0)
        d = d + jnp.sum(jnp.where(hit, v, 0.0).reshape(R // 8, 8, N), axis=0)
        return a, d

    zero = jnp.zeros((8, N), F32)
    col_dot, diag = lax.fori_loop(0, 16, dots_body, (zero, zero))
    col_dot = jnp.sum(col_dot, axis=0, keepdims=True)
    diag = jnp.sum(diag)

    for c in plane:
        c.wait_recv()
    to_cols(cols_b, merge(rst))
    to_rel(iabs)
    row_sum = jnp.sum(cols_a[0:R, 0:1])
    row_max[...] = 0.5 * jnp.exp(row_max[...] - cols_a[...])
    for c in ring:
        c.wait_recv()
    to_cols(cols_b, merge(cst))
    to_rel(tabs)
    c8 = to_rows(cols_a)
    cl = jnp.concatenate([c8[b:b + 1, :] for b in range(NL)], axis=1)
    fc = 0.5 * jnp.exp(cm - cl)

    def weights_body(s, _):
        rows, hit = tile_rows(s)
        w = er[rows, :] * row_max[rows, 0:1] + ec[rows, :] * fc
        wh[rows, :], wl[rows, :] = split(jnp.where(hit, w - 1.0, w))
        return 0

    lax.fori_loop(0, 16, weights_body, 0)

    def transpose(b0, b1):
        def body(b, _):
            cs = pl.ds(pl.multiple_of(b * 128, 128), 128)
            wth[cs, :] = wh[:, cs].T
            wtl[cs, :] = wl[:, cs].T
            return 0
        lax.fori_loop(b0, b1, body, 0)

    def product(dst, ah, al, bh, bl, a, b):
        rows = slice(a * R, b * R)

        def body(n, _):
            cs = pl.ds(pl.multiple_of(n * (E // 2), 128), E // 2)
            dst[rows, cs] = dot3(ah[rows, :], al[rows, :], bh[:, cs], bl[:, cs], ((1,), (0,)))
            return 0
        lax.fori_loop(0, 2, body, 0)

    def image_product(a, b):
        product(gi, wh, wl, th, tl, a, b)

    def text_product(a, b):
        product(gt, wth, wtl, ih, il, a, b)

    COL = {"f": slice(0, E), "A": slice(0, EH), "B": slice(EH, E)}
    red = {}

    def grows(h, o):
        return ISLOT[o] * R + h * H

    def quarter(h, p):
        o = pos(h, p, 2)
        r = pl.ds(grows(h, o), H)
        red[("q", h, p, 1)] = send(gi.at[r, HALF["A"]], rq.at[h, p, 0], idir(h, False, 1))
        red[("q", h, p, 3)] = send(gi.at[r, HALF["B"]], rq.at[h, p, 1], idir(h, False, -1))

    def unit(h, p):
        for q, part, j, s in ((1, "A", 0, 1), (3, "B", 1, -1)):
            red.pop(("q", h, p, q)).wait_recv()
            a = grows(h, pos(h, p, q))
            gi[a:a + H, COL[part]] += rq[h, p, j]
            red[("u", h, p, q)] = send(gi.at[pl.ds(a, H), :], ru.at[h, p, j], idir(h, False, s))

    def gathered(h, p):
        a = grows(h, pos(h, p, 0))
        for q in (1, 3):
            red.pop(("u", h, p, q)).wait_recv()
        gi[a:a + H, :] += ru[h, p, 0] + ru[h, p, 1]

    def pquarter(h):
        r = pl.ds(grows(h, pos(h, 2, 0)), H)
        red[("pq", h, 1)] = send(gi.at[r, HALF["A"]], rpq.at[h, 0], idir(h, True, 1))
        red[("pq", h, 3)] = send(gi.at[r, HALF["B"]], rpq.at[h, 1], idir(h, True, -1))

    def punit(h):
        for p, part, j, s in ((1, "A", 0, 1), (3, "B", 1, -1)):
            red.pop(("pq", h, p)).wait_recv()
            a = grows(h, pos(h, p, 0))
            gi[a:a + H, COL[part]] += rpq[h, j]
            red[("pu", h, p)] = send(gi.at[pl.ds(a, H), :], rpu.at[h, j], idir(h, True, s))

    def image_out(h):
        for p in (1, 3):
            red.pop(("pu", h, p)).wait_recv()
        a = grows(h, (0, 0))
        out_i[h * H:(h + 1) * H, :] = scale * (gi[a:a + H, :] + (rpu[h, 0] + rpu[h, 1]))

    def core_send(dz):
        red[("c", dz)] = send(gt.at[pl.ds(TSLOT[(dz, 1)] * R, R), :], rc.at[dz], CORE)

    def core_add(dz):
        red.pop(("c", dz)).wait_recv()
        a = TSLOT[(dz, 0)] * R
        gt[a:a + R, :] += rc[dz]

    def zsend(dz, s, ch):
        a, n = CHUNK[ch]
        src = gt.at[pl.ds(TSLOT[(dz, 0)] * R + a, n), :]
        red[("z", (dz - s) % 8, s, ch)] = send(src, rz.at[dz, pl.ds(a, n), :], zdir(s))

    def zadd(dz, s, ch):
        red.pop(("z", dz, s, ch)).wait_recv()
        a, n = CHUNK[ch]
        g = TSLOT[(dz, 0)] * R + a
        gt[g:g + n, :] += rz[(dz + s) % 8, a:a + n, :]

    def zstep(d, j):
        for dz, s, ch in ((d, 1, (2, 0, 1)[j]), (8 - d, -1, (0, 2, 1)[j])):
            if d == 3:
                came = None if j == 0 else ch if j == 1 else ("p" if s == 1 else "m")
            else:
                came = ch
            if came is not None:
                zadd(dz % 8, s, came)
            if d > 0:
                zsend(dz, s, ch)

    transpose(NL - 1, NL)
    text_product(14, 16)
    core_send(4)
    image_product(11, 16)
    for p in (2, 3, 1):
        for h in (0, 1):
            quarter(h, p)
    core_add(4)
    for s, ch in ((1, 0), (-1, 2), (1, "p"), (-1, "m")):
        zsend(4, s, ch)
    transpose(NL // 2, NL - 1)
    text_product(10, 14)
    for dz in (3, 5):
        core_send(dz)
    for h in (0, 1):
        unit(h, 2)
    image_product(5, 11)
    for dz in (3, 5):
        core_add(dz)
    zstep(3, 0)
    for h in (0, 1):
        quarter(h, 0)
    zstep(3, 1)
    for p in (3, 1):
        for h in (0, 1):
            unit(h, p)
    zstep(3, 2)

    scale_part = (jnp.sum(row_max[:, 0:1] * row_dot[:, 0:1]) + jnp.sum(fc * col_dot) - diag) / batch
    col_sum = jnp.sum(jnp.where(lane_n < R, cl, 0.0))
    loss_part = (row_sum + col_sum - 2.0 * diag) / (2.0 * batch)
    sub8 = lax.broadcasted_iota(jnp.int32, (8, 128), 0)
    pst[me_p] = jnp.where(sub8 == 0, loss_part, jnp.where(sub8 == 1, scale_part, 0.0))
    plane = [send(pst.at[me_p], pst.at[me_p], o) for o in PLANE]

    transpose(0, NL // 2)
    text_product(6, 10)
    for dz in (2, 6):
        core_send(dz)
    image_product(0, 5)
    for dz in (2, 6):
        core_add(dz)
    zstep(2, 0)
    zstep(2, 1)
    for h in (0, 1):
        gathered(h, 2)
        pquarter(h)
    zstep(2, 2)
    for h in (0, 1):
        unit(h, 0)
    text_product(0, 6)
    for dz in (1, 7, 0):
        core_send(dz)
    for c in plane:
        c.wait_recv()
    zst[me_r] = jnp.sum(pst[...], axis=0)
    ring = [send(zst.at[me_r], zst.at[me_r], o) for o in RING]
    for dz in (1, 7, 0):
        core_add(dz)
    zstep(1, 0)
    zstep(1, 1)
    for h in (0, 1):
        gathered(h, 3)
        gathered(h, 1)
        punit(h)
    zstep(1, 2)
    for c in ring:
        c.wait_recv()
    out_s[...] = jnp.sum(zst[...], axis=0)
    for h in (0, 1):
        gathered(h, 0)
    for j in (0, 1, 2):
        zstep(0, j)
    out_t[...] = scale * gt[0:R, :]
    for h in (0, 1):
        image_out(h)
    for c in copies:
        c.wait_send()


def finish(gi, gt, s, out_i, out_t, out_loss, out_scale):
    out_i[...] = gi[...]
    out_t[...] = gt[...]
    out_loss[0] = jnp.max(s[0:1, 0:1])
    out_scale[0] = jnp.max(s[1:2, 0:1])


def per_device(image, text, log_scale):
    R, E = image.shape
    N = 16 * R
    batch = 256 * R
    H, EH = R // 2, E // 2
    vm = pltpu.VMEM
    vspec = pl.BlockSpec(memory_space=pltpu.VMEM)
    sspec = pl.BlockSpec(memory_space=pltpu.SMEM)
    hspec = pl.BlockSpec(memory_space=pltpu.HBM)
    one = jax.ShapeDtypeStruct((1,), F32)
    grad = jax.ShapeDtypeStruct((R, E), F32)
    gi, gt, s = pl.pallas_call(
        functools.partial(kernel, R, E, float(batch)),
        out_shape=(grad, grad, jax.ShapeDtypeStruct((8, 128), F32)),
        in_specs=[hspec, hspec, hspec],
        out_specs=(vspec, vspec, vspec),
        scratch_shapes=[
            vm((16, R, E), F32), vm((16, R, E), F32),
            vm((N, E), BF16), vm((N, E), BF16), vm((N, E), BF16), vm((N, E), BF16),
            vm((N, N), F32), vm((N, N), F32), vm((N, N), F32), vm((N, N), BF16), vm((N, N), BF16), vm((N, N), BF16), vm((N, N), BF16),
            vm((N, E), F32), vm((N, E), F32),
            vm((2, 4, 2, H, EH), F32), vm((2, 4, 2, H, E), F32),
            vm((2, 2, H, EH), F32), vm((2, 2, H, E), F32),
            vm((8, R, E), F32), vm((8, R, E), F32),
            vm((N, 128), F32), vm((N, 128), F32), vm((N, 128), F32), vm((N, 128), F32),
            vm((16, 8, 128), F32), vm((16, 8, 128), F32), vm((16, 8, 128), F32), vm((16, 8, 128), F32),
            pltpu.SMEM((1,), F32), pltpu.SMEM((16,), jnp.int32), pltpu.SemaphoreType.DMA((3,)),
            pltpu.SemaphoreType.DMA((N_COPIES,)), pltpu.SemaphoreType.DMA((N_COPIES,)),
        ],
        compiler_params=pltpu.CompilerParams(collective_id=0, has_side_effects=True, vmem_limit_bytes=54 * 2**20),
        cost_estimate=pl.CostEstimate(flops=18 * N * N * E, bytes_accessed=16 * R * E, transcendentals=6 * N * N),
    )(image, text, log_scale)
    out_i, out_t, loss, scale_grad = pl.pallas_call(
        finish,
        out_shape=(grad, grad, one, one),
        in_specs=[vspec, vspec, vspec],
        out_specs=(vspec, vspec, sspec, sspec),
    )(gi, gt, s)
    return loss, out_i, out_t, scale_grad


def solution(mesh):
    return jax.shard_map(
        per_device,
        mesh=mesh,
        in_specs=(P(("row", "col"), None), P(("col", "row"), None), P()),
        out_specs=(P(), P(("row", "col"), None), P(("col", "row"), None), P()),
        check_vma=False,
    )
```

```python
import functools

import jax
import jax.numpy as jnp
from jax import lax
from jax.experimental import pallas as pl
from jax.experimental.pallas import tpu as pltpu
from jax.sharding import PartitionSpec as P

MESH = pl.DeviceIdType.MESH
F32 = jnp.float32
BF16 = jnp.bfloat16

NX, NZ = 4, 8
IMG = [(0, 0), (3, 0), (1, 0), (0, 3), (0, 1),
       (3, 3), (3, 1), (1, 3), (1, 1), (0, 2), (2, 0),
       (3, 2), (2, 3), (1, 2), (2, 1), (2, 2)]
TXT = [(dz, dk) for dz in (0, 7, 1, 6, 2, 5, 3, 4) for dk in (0, 1)]
ISLOT = {p: i for i, p in enumerate(IMG)}
TSLOT = {p: i for i, p in enumerate(TXT)}
PLANE = [(x, y, 0, 0) for x in (2, 3, 1, 0) for y in (2, 3, 1, 0) if (x, y) != (0, 0)]
RING = [(0, 0, z, k) for z in (4, 3, 5, 2, 6, 1, 7, 0) for k in (1, 0) if (z, k) != (0, 0)]
NEXT = [(1, 0, 0, 0), (3, 0, 0, 0), (0, 1, 0, 0), (0, 3, 0, 0), (0, 0, 1, 0), (0, 0, 7, 0), (0, 0, 0, 1)]
N_COPIES = 208
CHUNK = {0: (0, 16), 1: (16, 16), 2: (32, 16), "p": (16, 8), "m": (24, 8)}


def position():
    r, c = lax.axis_index("row"), lax.axis_index("col")
    return c // 4, r // 4, ((r // 2) % 2) * 4 + c % 4, r % 2


def shard_of(image, x, y, z, k):
    row, col = (y * 2 + z // 4) * 2 + k, x * 4 + z % 4
    return row * 16 + col if image else col * 16 + row


def split(v):
    hi = v.astype(BF16)
    return hi, (v - hi.astype(F32)).astype(BF16)


def dot3(ah, al, bh, bl, dims):
    d = functools.partial(lax.dot_general, dimension_numbers=(dims, ((), ())), preferred_element_type=F32)
    m = ah.shape[0]
    t = d(jnp.concatenate([ah, al], axis=0), bh)
    return t[:m] + (t[m:] + d(ah, bl))


def kernel(R, E, batch, im, tx, ls_hbm, out_i, out_t, out_s,
           img, txt, ih, il, th, tl, lg, er, ec, wh, wl, wth, wtl, gi, gt,
           rq, ru, rpq, rpu, rz, rc, cols_a, cols_b, row_max, row_dot, rst, cst, pst, zst, ls, rid, lsem, ssem, rsem):
    H = R // 2
    EH = E // 2
    N = 16 * R
    x, y, z, k = position()

    def peer(o):
        px, py, pz, pk = (x + o[0]) % 4, (y + o[1]) % 4, (z + o[2]) % 8, (k + o[3]) % 2
        return ((py * 2 + pz // 4) * 2 + pk, px * 4 + pz % 4)

    copies = []

    def send(src, dst, o):
        i = len(copies)
        c = pltpu.make_async_remote_copy(src_ref=src, dst_ref=dst, send_sem=ssem.at[i], recv_sem=rsem.at[i],
                                         device_id=peer(o), device_id_type=MESH)
        c.start()
        copies.append(c)
        return c

    CORE = (0, 0, 0, 1)

    def zdir(s):
        return (0, 0, s % 8, 0)

    def idir(h, primary, s):
        return (s % 4, 0, 0, 0) if (h == 0) == primary else (0, s % 4, 0, 0)

    def pos(h, p, q):
        p, q = p % 4, q % 4
        return (p, q) if h == 0 else (q, p)

    HALF = {"f": pl.ds(0, E), "A": pl.ds(0, EH), "B": pl.ds(EH, EH)}

    barrier = pltpu.get_barrier_semaphore()
    for o in NEXT:
        pl.semaphore_signal(barrier, inc=1, device_id=peer(o), device_id_type=MESH)
    local = [pltpu.make_async_copy(im, img.at[0], lsem.at[0]), pltpu.make_async_copy(tx, txt.at[0], lsem.at[1]),
             pltpu.make_async_copy(ls_hbm, ls, lsem.at[2])]
    for c in local:
        c.start()
    for s, (dx, dy) in enumerate(IMG):
        rid[s] = shard_of(True, (x + dx) % 4, (y + dy) % 4, z, k) * R
    for c in local:
        c.wait()
    pl.semaphore_wait(barrier, len(NEXT))

    got = {}

    def isend(h, p, q, primary, s, part="f"):
        o = pos(h, p, q)
        rows = pl.ds(h * H, H)
        src = img.at[ISLOT[o], rows, HALF[part]]
        to = pos(h, p - s, q) if primary else pos(h, p, q - s)
        got[("i", h, to, part)] = send(src, img.at[ISLOT[to], rows, HALF[part]], idir(h, primary, s))

    def iwait(h, p, q):
        o = pos(h, p, q)
        for part in ("f", "A", "B"):
            c = got.pop(("i", h, o, part), None)
            if c is not None:
                c.wait_recv()

    def tsend(dz, s, ch):
        rows = pl.ds(*CHUNK[ch])
        to = (dz - s) % 8
        got[("t", to, ch)] = send(txt.at[TSLOT[(dz, 0)], rows, :], txt.at[TSLOT[(to, 0)], rows, :], zdir(s))

    def tpass(d, ch):
        for dz, s in ((8 - d, 1), (d, -1)):
            got.pop(("t", dz, ch)).wait_recv()
            nxt = ch if d < 3 else {(1, 0): 0, (1, 1): "p", (-1, 1): "m", (-1, 2): 2}.get((s, ch))
            if nxt is not None:
                tsend(dz, s, nxt)

    def tlast():
        for ch in (0, "p", "m", 2):
            got.pop(("t", 4, ch)).wait_recv()

    def tlast_core():
        for ch in (0, 2, "p", "m"):
            got.pop(("t", 4, ch)).wait_recv()
            rows = pl.ds(*CHUNK[ch])
            got[("c4", ch)] = send(txt.at[TSLOT[(4, 0)], rows, :], txt.at[TSLOT[(4, 1)], rows, :], CORE)

    def cwait4():
        for ch in (0, 2, "p", "m"):
            got.pop(("c4", ch)).wait_recv()

    def tcore(dz):
        got[("c", dz)] = send(txt.at[TSLOT[(dz, 0)]], txt.at[TSLOT[(dz, 1)]], CORE)

    def cwait(dz):
        got.pop(("c", dz)).wait_recv()

    def put(hi_ref, lo_ref, s, v):
        rows = pl.ds(s * R if isinstance(s, int) else pl.multiple_of(s * R, R), R)
        hi_ref[rows, :], lo_ref[rows, :] = split(v)

    def conv(ref, hi_ref, lo_ref, a, b):
        def body(s, _):
            put(hi_ref, lo_ref, s, ref[s])
            return 0
        lax.fori_loop(a, b, body, 0)

    scale = jnp.exp(jnp.full((1, 1), ls[0], F32))

    def logits(a, b, t0, t1):
        rows = slice(a * R, b * R)

        def body(t, _):
            cs = pl.ds(pl.multiple_of(t * 256, 256), 256)
            lg[rows, cs] = scale * dot3(ih[rows, :], il[rows, :], th[cs, :], tl[cs, :], ((1,), (1,)))
            return 0
        lax.fori_loop(t0, t1, body, 0)

    def ipass(h, p, q, primary, s):
        isend(h, p, q, primary, s, "A" if s == 1 else "B")

    def second(p):
        for h in (0, 1):
            iwait(h, p, 3)
            ipass(h, p, 3, False, 1)
            iwait(h, p, 1)
            ipass(h, p, 1, False, -1)

    def third(p):
        for h in (0, 1):
            iwait(h, p, 2)

    for h in (0, 1):
        isend(h, 0, 0, True, 1)
        isend(h, 0, 0, True, -1)
    for ch in (0, 1, 2):
        tsend(0, 1, ch)
        tsend(0, -1, ch)
    for h in (0, 1):
        isend(h, 0, 0, False, 1)
        isend(h, 0, 0, False, -1)
    tcore(0)
    put(ih, il, 0, img[0])
    put(th, tl, 0, txt[0])

    tpass(1, 0)
    for h in (0, 1):
        iwait(h, 3, 0)
        ipass(h, 3, 0, True, 1)
        iwait(h, 1, 0)
        ipass(h, 1, 0, True, -1)
    for p in (3, 1):
        for h in (0, 1):
            isend(h, p, 0, False, 1)
            isend(h, p, 0, False, -1)
    tpass(1, 1)
    second(0)
    tpass(1, 2)
    tcore(7)
    tcore(1)
    for h in (0, 1):
        iwait(h, 2, 0)
        isend(h, 2, 0, False, 1)
        isend(h, 2, 0, False, -1)
    conv(img, ih, il, 1, 5)
    tpass(2, 0)
    for dz in (0, 7, 1):
        cwait(dz)
    conv(txt, th, tl, 1, 6)
    tpass(2, 1)
    logits(0, 5, 0, 1)
    second(3)
    tpass(2, 2)
    tcore(6)
    tcore(2)
    second(1)
    tpass(3, 0)
    cwait(6)
    cwait(2)
    conv(img, ih, il, 5, 9)
    third(0)
    tpass(3, 1)
    conv(txt, th, tl, 6, 10)
    second(2)
    tpass(3, 2)
    tcore(5)
    tcore(3)
    conv(img, ih, il, 9, 11)
    logits(5, 11, 0, 1)
    third(3)
    cwait(5)
    cwait(3)
    conv(txt, th, tl, 10, 14)
    logits(0, 11, 1, 2)
    tlast_core()
    third(1)
    conv(img, ih, il, 11, 15)
    logits(11, 15, 0, 2)
    cwait4()
    conv(txt, th, tl, 14, 16)
    logits(0, 15, 2, 3)
    third(2)
    conv(img, ih, il, 15, 16)
    logits(15, 16, 0, 3)

    RB = 2 * R
    NB = N // RB

    def rows_body(i, cm):
        rows = pl.ds(pl.multiple_of(i * RB, RB), RB)
        v = lg[rows, :]
        rm = jnp.max(v, axis=1, keepdims=True)
        e = jnp.exp(v - rm)
        er[rows, :] = e
        row_max[rows, :] = jnp.broadcast_to(rm, (RB, 128))
        rl = rm + jnp.log(jnp.sum(e, axis=1, keepdims=True))
        cols_a[rows, :] = jnp.broadcast_to(rl, (RB, 128))
        return jnp.maximum(cm, jnp.max(v.reshape(RB // 8, 8, N), axis=0))

    cm = lax.fori_loop(0, NB, rows_body, jnp.full((8, N), -jnp.inf, F32))
    cm = jnp.max(cm, axis=0, keepdims=True)

    def cols_body(i, cs):
        rows = pl.ds(pl.multiple_of(i * RB, RB), RB)
        e = jnp.exp(lg[rows, :] - cm)
        ec[rows, :] = e
        return cs + jnp.sum(e.reshape(RB // 8, 8, N), axis=0)

    NL = N // 128
    lane = lax.broadcasted_iota(jnp.int32, (128, 128), 1)

    def to_rows(ref):
        m = jnp.zeros((128, 128), F32)
        for b in range(NL):
            m = jnp.where(lane == b, ref[b * 128:(b + 1) * 128, :], m)
        return m.T[:8, :]

    def to_cols(ref, v):
        m = jnp.concatenate([v, jnp.zeros((120, 128), F32)], axis=0).T
        for b in range(NL):
            ref[b * 128:(b + 1) * 128, :] = jnp.broadcast_to(m[:, b:b + 1], (128, 128))

    def iabs(s):
        return ((x + IMG[s][0]) % 4) * 4 + (y + IMG[s][1]) % 4

    def tabs(s):
        return ((z + TXT[s][0]) % 8) * 2 + (k + TXT[s][1]) % 2

    def to_abs(where):
        for s in range(16):
            cols_b[pl.ds(pl.multiple_of(where(s) * R, R), R), :] = cols_a[s * R:(s + 1) * R, :]

    def to_rel(where):
        for s in range(16):
            cols_a[s * R:(s + 1) * R, :] = cols_b[pl.ds(pl.multiple_of(where(s) * R, R), R), :]

    me_p, me_r = x * 4 + y, z * 2 + k
    to_abs(iabs)
    rst[me_p] = to_rows(cols_b)
    plane = [send(rst.at[me_p], rst.at[me_p], o) for o in PLANE]
    cs = lax.fori_loop(0, NB, cols_body, jnp.zeros((8, N), F32))
    cl = cm + jnp.log(jnp.sum(cs, axis=0, keepdims=True))
    c8 = jnp.concatenate([cl[:, b * 128:(b + 1) * 128] for b in range(NL)] + [jnp.zeros((8 - NL, 128), F32)], axis=0)
    to_cols(cols_a, c8)
    to_abs(tabs)
    cst[me_r] = to_rows(cols_b)
    ring = [send(cst.at[me_r], cst.at[me_r], o) for o in RING]

    def merge(ref):
        v = ref[...]
        m = jnp.max(v, axis=0)
        return m + jnp.log(jnp.sum(jnp.exp(v - m[None]), axis=0))

    lane_n = lax.broadcasted_iota(jnp.int32, (1, N), 1)
    cid = lane_n
    for s, (dz, dk) in enumerate(TXT):
        base = shard_of(False, x, y, (z + dz) % 8, (k + dk) % 2) * R - s * R
        cid = jnp.where((lane_n >= s * R) & (lane_n < (s + 1) * R), lane_n + base, cid)

    sub = lax.broadcasted_iota(jnp.int32, (R, N), 0)

    def tile_rows(s):
        rows = pl.ds(pl.multiple_of(s * R, R), R)
        return rows, (cid - rid[s]) == sub

    def dots_body(s, c):
        rows, hit = tile_rows(s)
        v = lg[rows, :]
        a, d = c
        row_dot[rows, :] = jnp.broadcast_to(jnp.sum(er[rows, :] * v, axis=1, keepdims=True), (R, 128))
        a = a + jnp.sum((ec[rows, :] * v).reshape(R // 8, 8, N), axis=0)
        d = d + jnp.sum(jnp.where(hit, v, 0.0).reshape(R // 8, 8, N), axis=0)
        return a, d

    zero = jnp.zeros((8, N), F32)
    col_dot, diag = lax.fori_loop(0, 16, dots_body, (zero, zero))
    col_dot = jnp.sum(col_dot, axis=0, keepdims=True)
    diag = jnp.sum(diag)

    for c in plane:
        c.wait_recv()
    to_cols(cols_b, merge(rst))
    to_rel(iabs)
    row_sum = jnp.sum(cols_a[0:R, 0:1])
    row_max[...] = 0.5 * jnp.exp(row_max[...] - cols_a[...])
    for c in ring:
        c.wait_recv()
    to_cols(cols_b, merge(cst))
    to_rel(tabs)
    c8 = to_rows(cols_a)
    cl = jnp.concatenate([c8[b:b + 1, :] for b in range(NL)], axis=1)
    fc = 0.5 * jnp.exp(cm - cl)

    def weights_body(s, _):
        rows, hit = tile_rows(s)
        w = er[rows, :] * row_max[rows, 0:1] + ec[rows, :] * fc
        wh[rows, :], wl[rows, :] = split(jnp.where(hit, w - 1.0, w))
        return 0

    lax.fori_loop(0, 16, weights_body, 0)

    def transpose(b0, b1):
        def body(b, _):
            cs = pl.ds(pl.multiple_of(b * 128, 128), 128)
            wth[cs, :] = wh[:, cs].T
            wtl[cs, :] = wl[:, cs].T
            return 0
        lax.fori_loop(b0, b1, body, 0)

    def product(dst, ah, al, bh, bl, a, b):
        rows = slice(a * R, b * R)

        def body(n, _):
            cs = pl.ds(pl.multiple_of(n * (E // 2), 128), E // 2)
            dst[rows, cs] = dot3(ah[rows, :], al[rows, :], bh[:, cs], bl[:, cs], ((1,), (0,)))
            return 0
        lax.fori_loop(0, 2, body, 0)

    def image_product(a, b):
        product(gi, wh, wl, th, tl, a, b)

    def text_product(a, b):
        product(gt, wth, wtl, ih, il, a, b)

    COL = {"f": slice(0, E), "A": slice(0, EH), "B": slice(EH, E)}
    red = {}

    def grows(h, o):
        return ISLOT[o] * R + h * H

    def quarter(h, p):
        o = pos(h, p, 2)
        r = pl.ds(grows(h, o), H)
        red[("q", h, p, 1)] = send(gi.at[r, HALF["A"]], rq.at[h, p, 0], idir(h, False, 1))
        red[("q", h, p, 3)] = send(gi.at[r, HALF["B"]], rq.at[h, p, 1], idir(h, False, -1))

    def unit(h, p):
        for q, part, j, s in ((1, "A", 0, 1), (3, "B", 1, -1)):
            red.pop(("q", h, p, q)).wait_recv()
            a = grows(h, pos(h, p, q))
            gi[a:a + H, COL[part]] += rq[h, p, j]
            red[("u", h, p, q)] = send(gi.at[pl.ds(a, H), :], ru.at[h, p, j], idir(h, False, s))

    def gathered(h, p):
        a = grows(h, pos(h, p, 0))
        for q in (1, 3):
            red.pop(("u", h, p, q)).wait_recv()
        gi[a:a + H, :] += ru[h, p, 0] + ru[h, p, 1]

    def pquarter(h):
        r = pl.ds(grows(h, pos(h, 2, 0)), H)
        red[("pq", h, 1)] = send(gi.at[r, HALF["A"]], rpq.at[h, 0], idir(h, True, 1))
        red[("pq", h, 3)] = send(gi.at[r, HALF["B"]], rpq.at[h, 1], idir(h, True, -1))

    def punit(h):
        for p, part, j, s in ((1, "A", 0, 1), (3, "B", 1, -1)):
            red.pop(("pq", h, p)).wait_recv()
            a = grows(h, pos(h, p, 0))
            gi[a:a + H, COL[part]] += rpq[h, j]
            red[("pu", h, p)] = send(gi.at[pl.ds(a, H), :], rpu.at[h, j], idir(h, True, s))

    def image_out(h):
        for p in (1, 3):
            red.pop(("pu", h, p)).wait_recv()
        a = grows(h, (0, 0))
        out_i[h * H:(h + 1) * H, :] = scale * (gi[a:a + H, :] + (rpu[h, 0] + rpu[h, 1]))

    def core_send(dz):
        red[("c", dz)] = send(gt.at[pl.ds(TSLOT[(dz, 1)] * R, R), :], rc.at[dz], CORE)

    def core_add(dz):
        red.pop(("c", dz)).wait_recv()
        a = TSLOT[(dz, 0)] * R
        gt[a:a + R, :] += rc[dz]

    def zsend(dz, s, ch):
        a, n = CHUNK[ch]
        src = gt.at[pl.ds(TSLOT[(dz, 0)] * R + a, n), :]
        red[("z", (dz - s) % 8, s, ch)] = send(src, rz.at[dz, pl.ds(a, n), :], zdir(s))

    def zadd(dz, s, ch):
        red.pop(("z", dz, s, ch)).wait_recv()
        a, n = CHUNK[ch]
        g = TSLOT[(dz, 0)] * R + a
        gt[g:g + n, :] += rz[(dz + s) % 8, a:a + n, :]

    def zstep(d, j):
        for dz, s, ch in ((d, 1, (2, 0, 1)[j]), (8 - d, -1, (0, 2, 1)[j])):
            if d == 3:
                came = None if j == 0 else ch if j == 1 else ("p" if s == 1 else "m")
            else:
                came = ch
            if came is not None:
                zadd(dz % 8, s, came)
            if d > 0:
                zsend(dz, s, ch)

    transpose(NL - 1, NL)
    text_product(14, 16)
    core_send(4)
    image_product(11, 16)
    for p in (2, 3, 1):
        for h in (0, 1):
            quarter(h, p)
    core_add(4)
    for s, ch in ((1, 0), (-1, 2), (1, "p"), (-1, "m")):
        zsend(4, s, ch)
    transpose(NL // 2, NL - 1)
    text_product(10, 14)
    for dz in (3, 5):
        core_send(dz)
    for h in (0, 1):
        unit(h, 2)
    image_product(5, 11)
    for dz in (3, 5):
        core_add(dz)
    zstep(3, 0)
    for h in (0, 1):
        quarter(h, 0)
    zstep(3, 1)
    for p in (3, 1):
        for h in (0, 1):
            unit(h, p)
    zstep(3, 2)

    transpose(0, NL // 2)
    text_product(6, 10)
    for dz in (2, 6):
        core_send(dz)

    scale_part = (jnp.sum(row_max[:, 0:1] * row_dot[:, 0:1]) + jnp.sum(fc * col_dot) - diag) / batch
    col_sum = jnp.sum(jnp.where(lane_n < R, cl, 0.0))
    loss_part = (row_sum + col_sum - 2.0 * diag) / (2.0 * batch)
    sub8 = lax.broadcasted_iota(jnp.int32, (8, 128), 0)
    pst[me_p] = jnp.where(sub8 == 0, loss_part, jnp.where(sub8 == 1, scale_part, 0.0))
    plane = [send(pst.at[me_p], pst.at[me_p], o) for o in PLANE]

    image_product(0, 5)
    for dz in (2, 6):
        core_add(dz)
    zstep(2, 0)
    zstep(2, 1)
    for h in (0, 1):
        gathered(h, 2)
        pquarter(h)
    zstep(2, 2)
    for h in (0, 1):
        unit(h, 0)
    text_product(0, 6)
    for dz in (1, 7, 0):
        core_send(dz)
    for c in plane:
        c.wait_recv()
    zst[me_r] = jnp.sum(pst[...], axis=0)
    ring = [send(zst.at[me_r], zst.at[me_r], o) for o in RING]
    for dz in (1, 7, 0):
        core_add(dz)
    zstep(1, 0)
    zstep(1, 1)
    for h in (0, 1):
        gathered(h, 3)
        gathered(h, 1)
        punit(h)
    zstep(1, 2)
    for c in ring:
        c.wait_recv()
    out_s[...] = jnp.sum(zst[...], axis=0)
    for h in (0, 1):
        gathered(h, 0)
    for j in (0, 1, 2):
        zstep(0, j)
    out_t[...] = scale * gt[0:R, :]
    for h in (0, 1):
        image_out(h)
    for c in copies:
        c.wait_send()


def finish(gi, gt, s, out_i, out_t, out_loss, out_scale):
    out_i[...] = gi[...]
    out_t[...] = gt[...]
    out_loss[0] = jnp.max(s[0:1, 0:1])
    out_scale[0] = jnp.max(s[1:2, 0:1])


def per_device(image, text, log_scale):
    R, E = image.shape
    N = 16 * R
    batch = 256 * R
    H, EH = R // 2, E // 2
    vm = pltpu.VMEM
    vspec = pl.BlockSpec(memory_space=pltpu.VMEM)
    sspec = pl.BlockSpec(memory_space=pltpu.SMEM)
    hspec = pl.BlockSpec(memory_space=pltpu.HBM)
    one = jax.ShapeDtypeStruct((1,), F32)
    grad = jax.ShapeDtypeStruct((R, E), F32)
    gi, gt, s = pl.pallas_call(
        functools.partial(kernel, R, E, float(batch)),
        out_shape=(grad, grad, jax.ShapeDtypeStruct((8, 128), F32)),
        in_specs=[hspec, hspec, hspec],
        out_specs=(vspec, vspec, vspec),
        scratch_shapes=[
            vm((16, R, E), F32), vm((16, R, E), F32),
            vm((N, E), BF16), vm((N, E), BF16), vm((N, E), BF16), vm((N, E), BF16),
            vm((N, N), F32), vm((N, N), F32), vm((N, N), F32), vm((N, N), BF16), vm((N, N), BF16), vm((N, N), BF16), vm((N, N), BF16),
            vm((N, E), F32), vm((N, E), F32),
            vm((2, 4, 2, H, EH), F32), vm((2, 4, 2, H, E), F32),
            vm((2, 2, H, EH), F32), vm((2, 2, H, E), F32),
            vm((8, R, E), F32), vm((8, R, E), F32),
            vm((N, 128), F32), vm((N, 128), F32), vm((N, 128), F32), vm((N, 128), F32),
            vm((16, 8, 128), F32), vm((16, 8, 128), F32), vm((16, 8, 128), F32), vm((16, 8, 128), F32),
            pltpu.SMEM((1,), F32), pltpu.SMEM((16,), jnp.int32), pltpu.SemaphoreType.DMA((3,)),
            pltpu.SemaphoreType.DMA((N_COPIES,)), pltpu.SemaphoreType.DMA((N_COPIES,)),
        ],
        compiler_params=pltpu.CompilerParams(collective_id=0, has_side_effects=True, vmem_limit_bytes=54 * 2**20),
        cost_estimate=pl.CostEstimate(flops=18 * N * N * E, bytes_accessed=16 * R * E, transcendentals=6 * N * N),
    )(image, text, log_scale)
    out_i, out_t, loss, scale_grad = pl.pallas_call(
        finish,
        out_shape=(grad, grad, one, one),
        in_specs=[vspec, vspec, vspec],
        out_specs=(vspec, vspec, sspec, sspec),
    )(gi, gt, s)
    return loss, out_i, out_t, scale_grad


def solution(mesh):
    return jax.shard_map(
        per_device,
        mesh=mesh,
        in_specs=(P(("row", "col"), None), P(("col", "row"), None), P()),
        out_specs=(P(), P(("row", "col"), None), P(("col", "row"), None), P()),
        check_vma=False,
    )
```
